512 devices in a mesh: fsdp: 64 (over x_lo, z, core), tensor: 8 (over y, x_hi).
Axes of the slice: x: 4 (x_hi: 2, x_lo: 2; x = x_hi * 2 + x_lo), y: 4, z: 16, core: 2. Of those that a mesh axis runs over, the one named last changes fastest.
Arguments:
- tokens: bfloat16 [1344, 8192], P(None, 'tensor'), may hold values from -6 to 6
- gate_level_index: int32 [16384, 8192], P(('fsdp', 'tensor')), may hold values from 0 to 15
- upward_level_index: int32 [16384, 8192], P(('fsdp', 'tensor')), may hold values from 0 to 15
- gate_block_powers: int32 [16384, 128], P(('fsdp', 'tensor')), may hold values from -8 to -4
- upward_block_powers: int32 [16384, 128], P(('fsdp', 'tensor')), may hold values from -8 to -4
- gate_adapter_upward: bfloat16 [16384, 128], P(('fsdp', 'tensor')), may hold values from -0.5 to 0.5
- upward_adapter_upward: bfloat16 [16384, 128], P(('fsdp', 'tensor')), may hold values from -0.5 to 0.5
- gate_adapter_down: bfloat16 [128, 8192], P('fsdp', 'tensor'), may hold values from -0.0625 to 0.0625
- upward_adapter_down: bfloat16 [128, 8192], P('fsdp', 'tensor'), may hold values from -0.0625 to 0.0625
Outputs:
- activated: bfloat16 [1344, 16384], P('tensor', 'fsdp')
The draws below stay inside these ranges and needn't reach their ends.
All inputs are finite; a program needn't handle non-finite values.
Results may differ from the reference program's by a relative error of at most 0.023.
Values may be sent and summed in bfloat16 or wider, within the bound.
No kernel may reach another device: no remote copies, remote signals or barrier semaphores. Data moves between devices by JAX's collectives and lax.ppermute only.
A program may use at most 64 MiB of HBM per device.

```python
import jax
import jax.numpy as jnp
from jax import lax

MODEL_WIDTH = 8192
HIDDEN_SHARE = 16384
ADAPTER_RANK = 128
BLOCK = 64
TOKENS = 1344
N_TENSOR = 8


def touch_ends(values, own_key, least, largest):
    shape = values.shape
    index_at = [jax.random.randint(jax.random.fold_in(own_key, axis), (), 0, shape[axis]) for axis in range(len(shape))]
    values = values.at[tuple(index_at)].set(least)
    longest = shape.index(max(shape))
    index_at[longest] = (index_at[longest] + 1) % shape[longest]
    return values.at[tuple(index_at)].set(largest)


def steps_of(key, dims, split, least, high):
    loudness, own = 1.0, jax.random.fold_in(key, 6)
    for dim, blocks in split:
        steps = jnp.exp(jax.random.uniform(jax.random.fold_in(own, dim), (blocks,), jnp.float32, least / len(split), high / len(split)))
        loudness = loudness * jnp.repeat(steps, dims[dim] // blocks).reshape([-1 if axis == dim else 1 for axis in range(len(dims))])
    return loudness


def normal_values(rng, extent, deviation, limit, split=(), held_as=jnp.bfloat16):
    values = jax.random.normal(rng, extent, jnp.float32) * deviation
    if len(split) > 0:
        values = steps_of(rng, extent, split, -0.22, 0.18) * values
    return jnp.clip(values, min=-limit, max=limit).astype(held_as)


def setup_inputs(seed: int = 0) -> dict:
    streams_of = jax.random.split(jax.random.key(seed), 10)
    return {
        "tokens": normal_values(streams_of[0], (TOKENS, MODEL_WIDTH), 1.0, 6.0, ((1, 8),)),
        "gate_level_index": touch_ends(jax.random.randint(streams_of[1], (HIDDEN_SHARE, MODEL_WIDTH), 0, 16), jax.random.fold_in(streams_of[1], 1), 0, 15).astype(jnp.int32),
        "upward_level_index": touch_ends(jax.random.randint(streams_of[2], (HIDDEN_SHARE, MODEL_WIDTH), 0, 16), jax.random.fold_in(streams_of[2], 1), 0, 15).astype(jnp.int32),
        "gate_block_powers": touch_ends(jax.random.randint(streams_of[3], (HIDDEN_SHARE, MODEL_WIDTH // BLOCK), -8, -3), jax.random.fold_in(streams_of[3], 1), -8, (-3) - 1).astype(jnp.int32),
        "upward_block_powers": touch_ends(jax.random.randint(streams_of[4], (HIDDEN_SHARE, MODEL_WIDTH // BLOCK), -8, -3), jax.random.fold_in(streams_of[4], 1), -8, (-3) - 1).astype(jnp.int32),
        "gate_adapter_upward": normal_values(streams_of[5], (HIDDEN_SHARE, ADAPTER_RANK), ADAPTER_RANK ** -0.5, 0.5, ((0, 512),)),
        "upward_adapter_upward": normal_values(streams_of[6], (HIDDEN_SHARE, ADAPTER_RANK), ADAPTER_RANK ** -0.5, 0.5, ((0, 512),)),
        "gate_adapter_down": normal_values(streams_of[7], (ADAPTER_RANK, MODEL_WIDTH), MODEL_WIDTH ** -0.5, 0.0625, ((0, 64), (1, 8))),
        "upward_adapter_down": normal_values(streams_of[8], (ADAPTER_RANK, MODEL_WIDTH), MODEL_WIDTH ** -0.5, 0.0625, ((0, 64), (1, 8))),
    }


NF4_LEVELS = (-1.0, -0.6961928009986877, -0.5250730514526367, -0.39491748809814453,
              -0.28444138169288635, -0.18477343022823334, -0.09105003625154495, 0.0,
              0.07958029955625534, 0.16093020141124725, 0.24611230194568634, 0.33791524089813232,
              0.44070982933044434, 0.5626170039176941, 0.7229568362236023, 1.0)
adapter_scale = 1.0


def level_table():
    table = jnp.asarray(NF4_LEVELS, jnp.float32).astype(jnp.bfloat16)
    table = lax.optimization_barrier(table)
    return table.astype(jnp.float32)


def decode_quantized(codes, exponents):
    table = level_table()
    values = jnp.zeros(codes.shape, jnp.float32)
    for level in range(16):
        values = values + jnp.where(codes == level, table[level], 0.0)
    scales = jnp.exp2(exponents.astype(jnp.float32))
    nrows, ncols = codes.shape
    blocked = values.reshape(nrows, ncols // BLOCK, BLOCK) * scales[:, :, None]
    return blocked.reshape(nrows, ncols).astype(jnp.bfloat16)


def combine_weight(base_matrix, factor_b, factor_a):
    adapter_update = jnp.dot(factor_b, factor_a, preferred_element_type=jnp.float32)
    return (base_matrix.astype(jnp.float32) + adapter_scale * adapter_update).astype(jnp.bfloat16)


def reference(tokens, gate_level_index, upward_level_index, gate_block_powers, upward_block_powers, gate_adapter_upward, upward_adapter_upward, gate_adapter_down, upward_adapter_down):
    blocks = 8
    width = MODEL_WIDTH // N_TENSOR
    features = tokens.astype(jnp.float32).reshape(TOKENS, N_TENSOR, width)

    def divide_rows(array):
        return array.reshape(blocks, array.shape[0] // blocks, array.shape[1])

    def project(weight):
        wide = weight.astype(jnp.float32).reshape(weight.shape[0], N_TENSOR, width)
        parts = jnp.einsum('tkd,fkd->ktf', features, wide).astype(jnp.bfloat16)
        parts = lax.optimization_barrier(parts)
        return jnp.sum(parts.astype(jnp.float32), axis=0)

    def one_block(items):
        gate_level_ids, upward_level_ids, gate_scale_powers, upward_scale_powers, gate_adapter_pair, upward_adapter_pair = items
        gate_matrix = combine_weight(decode_quantized(gate_level_ids, gate_scale_powers), gate_adapter_pair, gate_adapter_down)
        upward_matrix = combine_weight(decode_quantized(upward_level_ids, upward_scale_powers), upward_adapter_pair, upward_adapter_down)
        return (jax.nn.silu(project(gate_matrix)) * project(upward_matrix)).astype(jnp.bfloat16)

    stacked = lax.map(one_block, (divide_rows(gate_level_index), divide_rows(upward_level_index), divide_rows(gate_block_powers),
                                  divide_rows(upward_block_powers), divide_rows(gate_adapter_upward), divide_rows(upward_adapter_upward)))
    return jnp.transpose(stacked, (1, 0, 2)).reshape(TOKENS, HIDDEN_SHARE)
```

```python
import jax
import jax.numpy as jnp
import ml_dtypes
from jax import lax
from jax.experimental import pallas as pl
from jax.experimental.pallas import tpu as pltpu
from jax.sharding import Mesh
from jax.sharding import PartitionSpec as P

BLOCK = 64
RANK = 128
GROUPS = 8
ROWS = 32
WIDTH = 1024
TOKENS = 1344
LANES = 128

NF4_LEVELS = (
    -1.0,
    -0.6961928009986877,
    -0.5250730514526367,
    -0.39491748809814453,
    -0.28444138169288635,
    -0.18477343022823334,
    -0.09105003625154495,
    0.0,
    0.07958029955625534,
    0.16093020141124725,
    0.24611230194568634,
    0.3379152408981323,
    0.44070982933044434,
    0.5626170039176941,
    0.7229568362236023,
    1.0,
)
LEVELS = tuple(float(ml_dtypes.bfloat16(v)) for v in NF4_LEVELS)

FSDP = ("xl", "z", "c")
TENSOR = ("y", "xh")


def lookup(table, index):
    return jnp.take_along_axis(table, index, axis=1, mode="promise_in_bounds")


def decode_kernel(gate_ids, up_ids, gate_powers, up_powers, gate_b, up_b, out):
    group = pl.program_id(0)
    lane = lax.broadcasted_iota(jnp.int32, (ROWS, LANES), 1)
    table = jnp.zeros((ROWS, LANES), jnp.float32)
    for level, value in enumerate(LEVELS):
        table = jnp.where(lane == level, value, table)
    half = lane // BLOCK
    for p, (ids, powers, factor) in enumerate(((gate_ids, gate_powers, gate_b), (up_ids, up_powers, up_b))):
        scales = (jnp.int32(1) << (powers[...] + 8)).astype(jnp.float32) * 2.0**-8
        rows = pl.ds(p * ROWS, ROWS)
        for chunk in range(WIDTH // LANES):
            columns = pl.ds(chunk * LANES, LANES)
            level = lookup(table, ids[:, columns])
            scale = lookup(scales, half + (group * (WIDTH // BLOCK) + chunk * (LANES // BLOCK)))
            out[0, rows, columns] = (level * scale).astype(jnp.bfloat16)
        out[0, rows, pl.ds(WIDTH, RANK)] = factor[...]


def decode(gate_ids, up_ids, gate_powers, up_powers, gate_b, up_b):
    whole = pl.BlockSpec((ROWS, RANK), lambda k: (0, 0))
    ids = pl.BlockSpec((ROWS, WIDTH), lambda k: (0, k))
    return pl.pallas_call(
        decode_kernel,
        grid=(GROUPS,),
        in_specs=[ids, ids, whole, whole, whole, whole],
        out_specs=pl.BlockSpec((1, 2 * ROWS, WIDTH + RANK), lambda k: (k, 0, 0)),
        out_shape=jax.ShapeDtypeStruct((GROUPS, 2 * ROWS, WIDTH + RANK), jnp.bfloat16),
        cost_estimate=pl.CostEstimate(flops=2**21, bytes_accessed=3 * 2**20, transcendentals=0),
        name="decode",
    )(gate_ids, up_ids, gate_powers, up_powers, gate_b, up_b)


def project_kernel(weights, a, tokens, out, merged):
    @pl.when(pl.program_id(0) == 0)
    def _():
        rank = lax.broadcasted_iota(jnp.int32, (RANK, 2 * RANK), 0)
        place = lax.broadcasted_iota(jnp.int32, (RANK, 2 * RANK), 1)
        inner = place % 4
        slot = place // 4
        owner = (slot // 32) * 32 + (slot % 16) * 2 + (slot // 16) % 2
        for p in range(2):
            factor = weights[:, pl.ds(p * ROWS, ROWS), pl.ds(WIDTH, RANK)].reshape(GROUPS * ROWS, RANK)
            pick = (inner // 2 == p) & (owner * 2 + inner % 2 == rank)
            spread = jnp.dot(
                factor, pick.astype(jnp.float32).astype(jnp.bfloat16), preferred_element_type=jnp.float32
            ).astype(jnp.bfloat16)
            update = jnp.dot(spread, a[...], preferred_element_type=jnp.float32)
            base = weights[:, pl.ds(p * ROWS, ROWS), pl.ds(0, WIDTH)].reshape(GROUPS * ROWS, WIDTH)
            merged[pl.ds(p * GROUPS * ROWS, GROUPS * ROWS), :] = (base.astype(jnp.float32) + update).astype(
                jnp.bfloat16
            )

    out[...] = lax.dot_general(
        tokens[...], merged[...], (((1,), (1,)), ((), ())), preferred_element_type=jnp.float32
    ).astype(jnp.bfloat16)


def project(weights, a, tokens, steps=2):
    part = TOKENS // steps
    return pl.pallas_call(
        project_kernel,
        grid=(steps,),
        in_specs=[
            pl.BlockSpec(weights.shape, lambda i: (0, 0, 0)),
            pl.BlockSpec(a.shape, lambda i: (0, 0)),
            pl.BlockSpec((part, WIDTH), lambda i: (i, 0)),
        ],
        out_specs=pl.BlockSpec((part, 2 * GROUPS * ROWS), lambda i: (i, 0)),
        out_shape=jax.ShapeDtypeStruct((TOKENS, 2 * GROUPS * ROWS), jnp.bfloat16),
        scratch_shapes=[pltpu.VMEM((2 * GROUPS * ROWS, WIDTH), jnp.bfloat16)],
        compiler_params=pltpu.CompilerParams(vmem_limit_bytes=48 * 2**20),
        cost_estimate=pl.CostEstimate(flops=2 * TOKENS * 512 * 1024, bytes_accessed=6 * 2**20, transcendentals=0),
        name="project",
    )(weights, a, tokens)


def finish_kernel(parts, out):
    total = parts[0].astype(jnp.float32)
    for k in range(1, GROUPS):
        total = total + parts[k].astype(jnp.float32)
    half = GROUPS * ROWS
    gate, up = total[:, :half], total[:, half:]
    out[...] = (gate / (1.0 + jnp.exp(-gate)) * up).astype(jnp.bfloat16)


def finish(parts):
    rows, columns = parts.shape[1], parts.shape[2] // 2
    return pl.pallas_call(
        finish_kernel,
        out_shape=jax.ShapeDtypeStruct((rows, columns), jnp.bfloat16),
        compiler_params=pltpu.CompilerParams(vmem_limit_bytes=32 * 2**20),
        cost_estimate=pl.CostEstimate(flops=2**20, bytes_accessed=3 * 2**19, transcendentals=2**16),
        name="finish",
    )(parts)


def per_device(tokens, gate_ids, up_ids, gate_powers, up_powers, gate_b, up_b, gate_a, up_a):
    own_a = jnp.concatenate([gate_a, up_a], axis=0)
    copies = jnp.broadcast_to(own_a[None], (lax.axis_size("z"),) + own_a.shape)
    a = lax.all_to_all(copies, "z", 0, 0, tiled=True)
    blocks = decode(gate_ids, up_ids, gate_powers, up_powers, gate_b, up_b)
    weights = lax.all_to_all(blocks, TENSOR, 0, 0, tiled=True)
    a = lax.all_gather(a.reshape(-1, WIDTH), "c", axis=0, tiled=True)
    a = lax.all_gather(a, "xl", axis=0, tiled=True)
    parts = project(weights, a, tokens)
    parts = lax.all_to_all(parts.reshape(GROUPS, TOKENS // GROUPS, -1), TENSOR, 0, 0, tiled=True)
    return finish(parts)


def solution(mesh):
    split = Mesh(mesh.devices.reshape(2, 16, 2, 4, 2), ("xl", "z", "c", "y", "xh"))
    rows = P(FSDP + TENSOR, None)
    placed = (P(None, TENSOR), rows, rows, rows, rows, rows, rows, P(FSDP, TENSOR), P(FSDP, TENSOR))
    return jax.shard_map(per_device, mesh=split, in_specs=placed, out_specs=P(TENSOR, FSDP), check_vma=False)
```

```python
import jax
import jax.numpy as jnp
import ml_dtypes
from jax import lax
from jax.experimental import pallas as pl
from jax.experimental.pallas import tpu as pltpu
from jax.sharding import Mesh
from jax.sharding import PartitionSpec as P

BLOCK = 64
RANK = 128
GROUPS = 8
ROWS = 32
WIDTH = 1024
TOKENS = 1344
LANES = 128
PIECES = 2
SIDE = 144

NF4_LEVELS = (
    -1.0,
    -0.6961928009986877,
    -0.5250730514526367,
    -0.39491748809814453,
    -0.28444138169288635,
    -0.18477343022823334,
    -0.09105003625154495,
    0.0,
    0.07958029955625534,
    0.16093020141124725,
    0.24611230194568634,
    0.3379152408981323,
    0.44070982933044434,
    0.5626170039176941,
    0.7229568362236023,
    1.0,
)
LEVELS = tuple(float(ml_dtypes.bfloat16(v)) for v in NF4_LEVELS)

FSDP = ("xl", "z", "c")
TENSOR = ("y", "xh")
def pick(ids, low, high):
    if high - low == 1:
        return jnp.full(ids.shape, LEVELS[low], jnp.float32)
    middle = (low + high) // 2
    return jnp.where(ids < middle, pick(ids, low, middle), pick(ids, middle, high))


def lookup(table, index):
    return jnp.take_along_axis(table, index, axis=1, mode="promise_in_bounds")


def decode_kernel(gate_ids, up_ids, gate_powers, up_powers, gate_b, up_b, gate_a, up_a, out, ids, small, blocks, ready, near, sent):
    extra = [
        pltpu.make_async_copy(powers, small.at[p], near.at[p]) for p, powers in enumerate((gate_powers, up_powers))
    ]
    loads, stores = [], []
    for k in range(GROUPS):
        columns = pl.ds(k * WIDTH, WIDTH)
        loads.append(
            [pltpu.make_async_copy(ref.at[:, columns], ids.at[p, k], ready.at[p, k]) for p, ref in enumerate((gate_ids, up_ids))]
        )
    for copy in extra + sum(loads, []):
        copy.start()
    blocks[GROUPS, :, :] = jnp.zeros((2 * ROWS, WIDTH), jnp.bfloat16)
    blocks[GROUPS, pl.ds(0, ROWS), pl.ds(0, RANK)] = gate_b[...]
    blocks[GROUPS, pl.ds(ROWS, ROWS), pl.ds(0, RANK)] = up_b[...]
    blocks[GROUPS + 1, :, :] = jnp.zeros((2 * ROWS, WIDTH), jnp.bfloat16)
    blocks[GROUPS + 1, pl.ds(0, 2), :] = gate_a[...]
    blocks[GROUPS + 1, pl.ds(2, 2), :] = up_a[...]
    stores.append(pltpu.make_async_copy(blocks.at[pl.ds(GROUPS, 2)], out.at[pl.ds(GROUPS, 2)], sent.at[GROUPS]))
    stores[-1].start()
    for copy in extra:
        copy.wait()
    half = lax.broadcasted_iota(jnp.int32, (ROWS, LANES), 1) // BLOCK
    scales = [(jnp.int32(1) << (small[p] + 8)).astype(jnp.float32) * 2.0**-8 for p in range(2)]
    for k in range(GROUPS):
        for p in range(2):
            loads[k][p].wait()
            rows = pl.ds(p * ROWS, ROWS)
            for chunk in range(WIDTH // LANES):
                columns = pl.ds(chunk * LANES, LANES)
                level = pick(ids[p, k, :, columns], 0, len(LEVELS))
                scale = lookup(scales[p], half + (k * (WIDTH // BLOCK) + chunk * (LANES // BLOCK)))
                blocks[k, rows, columns] = (level * scale).astype(jnp.bfloat16)
        stores.append(pltpu.make_async_copy(blocks.at[k], out.at[k], sent.at[k]))
        stores[-1].start()
    for store in stores:
        store.wait()


def decode(*args):
    shape = (GROUPS + 2, 2 * ROWS, WIDTH)
    hbm, vmem = pl.BlockSpec(memory_space=pltpu.HBM), pl.BlockSpec(memory_space=pltpu.VMEM)
    return pl.pallas_call(
        decode_kernel,
        in_specs=[hbm] * 4 + [vmem] * 4,
        out_specs=hbm,
        out_shape=jax.ShapeDtypeStruct(shape, jnp.bfloat16),
        scratch_shapes=[
            pltpu.VMEM((2, GROUPS, ROWS, WIDTH), jnp.int32),
            pltpu.VMEM((2, ROWS, LANES), jnp.int32),
            pltpu.VMEM(shape, jnp.bfloat16),
            pltpu.SemaphoreType.DMA((2, GROUPS)),
            pltpu.SemaphoreType.DMA((2,)),
            pltpu.SemaphoreType.DMA((GROUPS + 1,)),
        ],
        compiler_params=pltpu.CompilerParams(vmem_limit_bytes=62 * 2**20),
        cost_estimate=pl.CostEstimate(flops=2**24, bytes_accessed=3 * 2**20, transcendentals=0),
        name="decode",
    )(*args)


def project_kernel(weights, tokens, out, merged, held, ready):
    part = TOKENS // PIECES
    loads = []
    for i in range(PIECES):
        loads.append(pltpu.make_async_copy(tokens.at[pl.ds(i * part, part)], held.at[pl.ds(i * part, part)], ready.at[i]))
        loads[-1].start()
    half = GROUPS * ROWS
    for q in range(4):
        merged[pl.ds(q * half, half), :] = weights[:, pl.ds(q * ROWS, ROWS), :].reshape(half, WIDTH)
    for i in range(PIECES):
        rows = pl.ds(i * part, part)
        loads[i].wait()
        for q in range(4):
            columns = pl.ds(q * half, half)
            out[rows, columns] = lax.dot_general(
                held[rows, :], merged[columns, :], (((1,), (1,)), ((), ())), preferred_element_type=jnp.float32
            ).astype(jnp.bfloat16)


def project(weights, tokens):
    place = pl.BlockSpec(memory_space=pltpu.VMEM)
    columns = 4 * GROUPS * ROWS
    return pl.pallas_call(
        project_kernel,
        in_specs=[place, pl.BlockSpec(memory_space=pltpu.HBM)],
        out_specs=place,
        out_shape=jax.ShapeDtypeStruct((TOKENS, columns), jnp.bfloat16),
        scratch_shapes=[
            pltpu.VMEM((columns, WIDTH), jnp.bfloat16),
            pltpu.VMEM((TOKENS, WIDTH), jnp.bfloat16),
            pltpu.SemaphoreType.DMA((PIECES,)),
        ],
        compiler_params=pltpu.CompilerParams(vmem_limit_bytes=40 * 2**20),
        cost_estimate=pl.CostEstimate(flops=2 * TOKENS * 1024 * 1024, bytes_accessed=8 * 2**20, transcendentals=0),
        name="project",
    )(weights, tokens)


def add_up_kernel(parts, mine, theirs):
    half = 2 * GROUPS * ROWS
    for to, columns in ((mine, pl.ds(0, half)), (theirs, pl.ds(half, half))):
        total = parts[0, :, columns].astype(jnp.float32)
        for k in range(1, GROUPS):
            total = total + parts[k, :, columns].astype(jnp.float32)
        to[...] = total


def add_up(parts):
    shape = jax.ShapeDtypeStruct((parts.shape[1], parts.shape[2] // 2), jnp.float32)
    return pl.pallas_call(
        add_up_kernel,
        out_shape=[shape, shape],
        compiler_params=pltpu.CompilerParams(vmem_limit_bytes=32 * 2**20),
        cost_estimate=pl.CostEstimate(flops=2**21, bytes_accessed=3 * 2**20, transcendentals=0),
        name="add_up",
    )(parts)


def shrink_kernel(first, second, tokens, out):
    a = jnp.concatenate([first[1, pl.ds(0, 4), :].astype(jnp.float32), second[1, pl.ds(0, 4), :].astype(jnp.float32)], axis=0)
    a = a.astype(jnp.bfloat16)
    count = TOKENS // GROUPS
    for k in range(GROUPS):
        out[k, pl.ds(0, 2 * ROWS), :] = first[0, :, pl.ds(0, RANK)]
        out[k, pl.ds(2 * ROWS, 2 * ROWS), :] = second[0, :, pl.ds(0, RANK)]
        product = lax.dot_general(a, tokens[k], (((1,), (1,)), ((), ())), preferred_element_type=jnp.float32)
        rest = jnp.concatenate([product[:, LANES:], jnp.zeros((8, 2 * LANES - count), jnp.float32)], axis=1)
        out[k, pl.ds(4 * ROWS, 16), :] = jnp.concatenate([product[:, :LANES], rest], axis=0).astype(jnp.bfloat16)


def shrink(first, second, tokens):
    side = pl.BlockSpec((2, 2 * ROWS, WIDTH), lambda i: (GROUPS // 2, 0, 0))
    return pl.pallas_call(
        shrink_kernel,
        grid=(1,),
        in_specs=[side, side, pl.BlockSpec((GROUPS, TOKENS // GROUPS, WIDTH), lambda i: (0, 0, 0))],
        out_specs=pl.BlockSpec((GROUPS, SIDE, LANES), lambda i: (0, 0, 0)),
        out_shape=jax.ShapeDtypeStruct((GROUPS, SIDE, LANES), jnp.bfloat16),
        compiler_params=pltpu.CompilerParams(vmem_limit_bytes=40 * 2**20),
        cost_estimate=pl.CostEstimate(flops=2**24, bytes_accessed=3 * 2**20, transcendentals=0),
        name="shrink",
    )(first, second, tokens.reshape(GROUPS, TOKENS // GROUPS, WIDTH))


def gather_kernel(side, out):
    total = side[0, pl.ds(4 * ROWS, 16), :].astype(jnp.float32)
    for k in range(1, GROUPS):
        total = total + side[k, pl.ds(4 * ROWS, 16), :].astype(jnp.float32)
    for z in range(out.shape[0]):
        out[z] = total.astype(jnp.bfloat16)


def copies_of(side, count):
    return pl.pallas_call(
        gather_kernel,
        out_shape=jax.ShapeDtypeStruct((count, 16, LANES), jnp.bfloat16),
        cost_estimate=pl.CostEstimate(flops=2**14, bytes_accessed=2**19, transcendentals=0),
        name="copies",
    )(side)


def grow_kernel(side, shrunk, mine, theirs):
    count = TOKENS // GROUPS
    rank = lax.broadcasted_iota(jnp.int32, (RANK, 2 * RANK), 0)
    place = lax.broadcasted_iota(jnp.int32, (RANK, 2 * RANK), 1)
    spreads = [
        ((place % 4 // 2 == p) & (place // 4 * 2 + place % 2 == rank)).astype(jnp.float32).astype(jnp.bfloat16) for p in range(2)
    ]
    values = shrunk[...].astype(jnp.float32)
    low = values[:, 0:8, :].reshape(2 * RANK, LANES).T.astype(jnp.bfloat16)
    high = values[:, 8:16, :].reshape(2 * RANK, LANES).T.astype(jnp.bfloat16)
    half = GROUPS * ROWS
    for q in range(4):
        factor = side[:, pl.ds(q * ROWS, ROWS), :].reshape(half, RANK)
        factor = jnp.dot(factor, spreads[q % 2], preferred_element_type=jnp.float32).astype(jnp.bfloat16)
        to = theirs if q < 2 else mine
        columns = pl.ds(q % 2 * half, half)
        to[pl.ds(0, LANES), columns] = lax.dot_general(
            low, factor, (((1,), (1,)), ((), ())), preferred_element_type=jnp.float32
        )
        to[pl.ds(LANES, count - LANES), columns] = lax.dot_general(
            high, factor, (((1,), (1,)), ((), ())), preferred_element_type=jnp.float32
        )[: count - LANES]


def grow(side, shrunk):
    shape = jax.ShapeDtypeStruct((TOKENS // GROUPS, 2 * GROUPS * ROWS), jnp.float32)
    return pl.pallas_call(
        grow_kernel,
        out_shape=[shape, shape],
        compiler_params=pltpu.CompilerParams(vmem_limit_bytes=32 * 2**20),
        cost_estimate=pl.CostEstimate(flops=2**25, bytes_accessed=2**20, transcendentals=0),
        name="grow",
    )(side, shrunk)


def finish_kernel(mine, other, out):
    half = GROUPS * ROWS
    gate = mine[:, :half] + other[:, :half]
    up = mine[:, half:] + other[:, half:]
    out[...] = (gate / (1.0 + jnp.exp(-gate)) * up).astype(jnp.bfloat16)


def finish(mine, other):
    return pl.pallas_call(
        finish_kernel,
        out_shape=jax.ShapeDtypeStruct((TOKENS // GROUPS, GROUPS * ROWS), jnp.bfloat16),
        compiler_params=pltpu.CompilerParams(vmem_limit_bytes=32 * 2**20),
        cost_estimate=pl.CostEstimate(flops=2**20, bytes_accessed=3 * 2**19, transcendentals=2**16),
        name="finish",
    )(mine, other)


def base_term(blocks, other, tokens):
    weights = jnp.concatenate([blocks[:GROUPS], other[:GROUPS]], axis=1)
    weights = lax.all_to_all(weights, TENSOR, 0, 0, tiled=True)
    parts = project(weights, tokens)
    parts = lax.all_to_all(parts.reshape(GROUPS, TOKENS // GROUPS, -1), TENSOR, 0, 0, tiled=True)
    return tuple(add_up(parts))


def adapter_term(blocks, other, tokens):
    side = lax.all_to_all(shrink(other, blocks, tokens), TENSOR, 0, 0, tiled=True)
    shrunk = lax.all_to_all(copies_of(side, lax.axis_size("z")), "z", 0, 0, tiled=True)
    shrunk = lax.all_gather(shrunk, "xl", axis=0, tiled=True)
    return tuple(grow(side, shrunk))


def per_device(tokens, gate_ids, up_ids, gate_powers, up_powers, gate_b, up_b, gate_a, up_a):
    blocks = decode(gate_ids, up_ids, gate_powers, up_powers, gate_b, up_b, gate_a, up_a)
    swap = [(0, 1), (1, 0)]
    other = lax.ppermute(blocks, "c", swap)
    mine, theirs = lax.cond(lax.axis_index("c") == 0, base_term, adapter_term, blocks, other, tokens)
    return finish(mine, lax.ppermute(theirs, "c", swap))


def solution(mesh):
    split = Mesh(mesh.devices.reshape(2, 16, 2, 4, 2), ("xl", "z", "c", "y", "xh"))
    rows = P(FSDP + TENSOR, None)
    placed = (P(None, TENSOR), rows, rows, rows, rows, rows, rows, P(FSDP, TENSOR), P(FSDP, TENSOR))
    return jax.shard_map(per_device, mesh=split, in_specs=placed, out_specs=P(TENSOR, FSDP), check_vma=False)
```

```python
import jax
import jax.numpy as jnp
import ml_dtypes
from jax import lax
from jax.experimental import pallas as pl
from jax.experimental.pallas import tpu as pltpu
from jax.sharding import Mesh
from jax.sharding import PartitionSpec as P

BLOCK = 64
RANK = 128
GROUPS = 8
ROWS = 32
WIDTH = 1024
TOKENS = 1344
LANES = 128
PIECES = 2
SIDE = 144

NF4_LEVELS = (
    -1.0,
    -0.6961928009986877,
    -0.5250730514526367,
    -0.39491748809814453,
    -0.28444138169288635,
    -0.18477343022823334,
    -0.09105003625154495,
    0.0,
    0.07958029955625534,
    0.16093020141124725,
    0.24611230194568634,
    0.3379152408981323,
    0.44070982933044434,
    0.5626170039176941,
    0.7229568362236023,
    1.0,
)
LEVELS = tuple(float(ml_dtypes.bfloat16(v)) for v in NF4_LEVELS)

FSDP = ("xl", "z", "c")
TENSOR = ("y", "xh")
def pick(ids, low, high):
    if high - low == 1:
        return jnp.full(ids.shape, LEVELS[low], jnp.bfloat16)
    middle = (low + high) // 2
    return jnp.where(ids < jnp.int16(middle), pick(ids, low, middle), pick(ids, middle, high))


def lookup(table, index):
    return jnp.take_along_axis(table, index, axis=1, mode="promise_in_bounds")


def decode_kernel(gate_ids, up_ids, gate_powers, up_powers, gate_b, up_b, gate_a, up_a, out, ids, small, thin, blocks, ready, near, sent):
    extra, stores = [], []
    for p, (powers, factor, a) in enumerate(((gate_powers, gate_b, gate_a), (up_powers, up_b, up_a))):
        extra.append(pltpu.make_async_copy(powers, small.at[p], near.at[p]))
        extra.append(pltpu.make_async_copy(a, thin.at[p], near.at[2 + p]))
        place = out.at[GROUPS, pl.ds(p * ROWS, ROWS), pl.ds(0, RANK)]
        stores.append(pltpu.make_async_copy(factor, place, sent.at[GROUPS + 1 + p]))
    loads = []
    for k in range(GROUPS):
        columns = pl.ds(k * WIDTH, WIDTH)
        loads.append(
            [pltpu.make_async_copy(ref.at[:, columns], ids.at[p, k], ready.at[p, k]) for p, ref in enumerate((gate_ids, up_ids))]
        )
    for copy in extra + sum(loads, []) + stores:
        copy.start()
    for copy in extra:
        copy.wait()
    rows = jnp.concatenate([thin[0].astype(jnp.float32), thin[1].astype(jnp.float32), jnp.zeros((12, WIDTH), jnp.float32)], axis=0)
    blocks[GROUPS, pl.ds(0, 16), :] = rows.astype(jnp.bfloat16)
    stores.append(
        pltpu.make_async_copy(blocks.at[GROUPS, pl.ds(0, 16)], out.at[GROUPS + 1, pl.ds(0, 16)], sent.at[GROUPS])
    )
    stores[-1].start()
    half = lax.broadcasted_iota(jnp.int32, (ROWS, LANES), 1) // BLOCK
    scales = [(jnp.int32(1) << (small[p] + 8)).astype(jnp.float32) * 2.0**-8 for p in range(2)]
    for k in range(GROUPS):
        for p in range(2):
            loads[k][p].wait()
            rows = pl.ds(p * ROWS, ROWS)
            for chunk in range(WIDTH // LANES):
                columns = pl.ds(chunk * LANES, LANES)
                level = pick(ids[p, k, :, columns].astype(jnp.int16), 0, len(LEVELS))
                scale = lookup(scales[p], half + (k * (WIDTH // BLOCK) + chunk * (LANES // BLOCK)))
                blocks[k, rows, columns] = level * scale.astype(jnp.bfloat16)
        stores.append(pltpu.make_async_copy(blocks.at[k], out.at[k], sent.at[k]))
        stores[-1].start()
    for store in stores:
        store.wait()


def decode(*args):
    shape = (GROUPS + 2, 2 * ROWS, WIDTH)
    hbm = pl.BlockSpec(memory_space=pltpu.HBM)
    return pl.pallas_call(
        decode_kernel,
        in_specs=[hbm] * 8,
        out_specs=hbm,
        out_shape=jax.ShapeDtypeStruct(shape, jnp.bfloat16),
        scratch_shapes=[
            pltpu.VMEM((2, GROUPS, ROWS, WIDTH), jnp.int32),
            pltpu.VMEM((2, ROWS, LANES), jnp.int32),
            pltpu.VMEM((2, 2, WIDTH), jnp.bfloat16),
            pltpu.VMEM((GROUPS + 1, 2 * ROWS, WIDTH), jnp.bfloat16),
            pltpu.SemaphoreType.DMA((2, GROUPS)),
            pltpu.SemaphoreType.DMA((4,)),
            pltpu.SemaphoreType.DMA((GROUPS + 3,)),
        ],
        compiler_params=pltpu.CompilerParams(vmem_limit_bytes=62 * 2**20),
        cost_estimate=pl.CostEstimate(flops=2**24, bytes_accessed=3 * 2**20, transcendentals=0),
        name="decode",
    )(*args)


def project_kernel(weights, tokens, out, merged, held, ready):
    part = TOKENS // PIECES
    loads = []
    for i in range(PIECES):
        loads.append(pltpu.make_async_copy(tokens.at[pl.ds(i * part, part)], held.at[pl.ds(i * part, part)], ready.at[i]))
        loads[-1].start()
    half = GROUPS * ROWS
    for q in range(4):
        merged[pl.ds(q * half, half), :] = weights[:, pl.ds(q * ROWS, ROWS), :].reshape(half, WIDTH)
    for i in range(PIECES):
        rows = pl.ds(i * part, part)
        loads[i].wait()
        for q in range(4):
            columns = pl.ds(q * half, half)
            out[rows, columns] = lax.dot_general(
                held[rows, :], merged[columns, :], (((1,), (1,)), ((), ())), preferred_element_type=jnp.float32
            ).astype(jnp.bfloat16)


def project(weights, tokens):
    place = pl.BlockSpec(memory_space=pltpu.VMEM)
    columns = 4 * GROUPS * ROWS
    return pl.pallas_call(
        project_kernel,
        in_specs=[place, pl.BlockSpec(memory_space=pltpu.HBM)],
        out_specs=place,
        out_shape=jax.ShapeDtypeStruct((TOKENS, columns), jnp.bfloat16),
        scratch_shapes=[
            pltpu.VMEM((columns, WIDTH), jnp.bfloat16),
            pltpu.VMEM((TOKENS, WIDTH), jnp.bfloat16),
            pltpu.SemaphoreType.DMA((PIECES,)),
        ],
        compiler_params=pltpu.CompilerParams(vmem_limit_bytes=40 * 2**20),
        cost_estimate=pl.CostEstimate(flops=2 * TOKENS * 1024 * 1024, bytes_accessed=8 * 2**20, transcendentals=0),
        name="project",
    )(weights, tokens)


def add_up_kernel(parts, mine, theirs):
    half = 2 * GROUPS * ROWS
    for to, columns in ((theirs, pl.ds(0, half)), (mine, pl.ds(half, half))):
        total = parts[0, :, columns].astype(jnp.float32)
        for k in range(1, GROUPS):
            total = total + parts[k, :, columns].astype(jnp.float32)
        to[...] = total


def add_up(parts):
    shape = jax.ShapeDtypeStruct((parts.shape[1], parts.shape[2] // 2), jnp.float32)
    return pl.pallas_call(
        add_up_kernel,
        out_shape=[shape, shape],
        compiler_params=pltpu.CompilerParams(vmem_limit_bytes=32 * 2**20),
        cost_estimate=pl.CostEstimate(flops=2**21, bytes_accessed=3 * 2**20, transcendentals=0),
        name="add_up",
    )(parts)


def shrink_kernel(first, second, tokens, out):
    a = jnp.concatenate([first[1, pl.ds(0, 4), :].astype(jnp.float32), second[1, pl.ds(0, 4), :].astype(jnp.float32)], axis=0)
    a = a.astype(jnp.bfloat16)
    count = TOKENS // GROUPS
    for k in range(GROUPS):
        out[k, pl.ds(0, 2 * ROWS), :] = first[0, :, pl.ds(0, RANK)]
        out[k, pl.ds(2 * ROWS, 2 * ROWS), :] = second[0, :, pl.ds(0, RANK)]
        product = lax.dot_general(a, tokens[k], (((1,), (1,)), ((), ())), preferred_element_type=jnp.float32)
        rest = jnp.concatenate([product[:, LANES:], jnp.zeros((8, 2 * LANES - count), jnp.float32)], axis=1)
        out[k, pl.ds(4 * ROWS, 16), :] = jnp.concatenate([product[:, :LANES], rest], axis=0).astype(jnp.bfloat16)


def shrink(first, second, tokens):
    side = pl.BlockSpec((2, 2 * ROWS, WIDTH), lambda i: (GROUPS // 2, 0, 0))
    return pl.pallas_call(
        shrink_kernel,
        grid=(1,),
        in_specs=[side, side, pl.BlockSpec((GROUPS, TOKENS // GROUPS, WIDTH), lambda i: (0, 0, 0))],
        out_specs=pl.BlockSpec((GROUPS, SIDE, LANES), lambda i: (0, 0, 0)),
        out_shape=jax.ShapeDtypeStruct((GROUPS, SIDE, LANES), jnp.bfloat16),
        compiler_params=pltpu.CompilerParams(vmem_limit_bytes=40 * 2**20),
        cost_estimate=pl.CostEstimate(flops=2**24, bytes_accessed=3 * 2**20, transcendentals=0),
        name="shrink",
    )(first, second, tokens.reshape(GROUPS, TOKENS // GROUPS, WIDTH))


def copies_kernel(side, out):
    total = side[0, pl.ds(4 * ROWS, 16), :].astype(jnp.float32)
    for k in range(1, GROUPS):
        total = total + side[k, pl.ds(4 * ROWS, 16), :].astype(jnp.float32)
    for place in range(out.shape[0]):
        out[place] = total.astype(jnp.bfloat16)


def copies_of(side, count):
    return pl.pallas_call(
        copies_kernel,
        out_shape=jax.ShapeDtypeStruct((count, 16, LANES), jnp.bfloat16),
        cost_estimate=pl.CostEstimate(flops=2**14, bytes_accessed=2**19, transcendentals=0),
        name="copies",
    )(side)


def spread_kernel(side, out):
    rank = lax.broadcasted_iota(jnp.int32, (RANK, 2 * RANK), 0)
    place = lax.broadcasted_iota(jnp.int32, (RANK, 2 * RANK), 1)
    for q in range(4):
        hit = (place % 4 // 2 == q % 2) & (place // 4 * 2 + place % 2 == rank)
        factor = side[:, pl.ds(q * ROWS, ROWS), :].reshape(GROUPS * ROWS, RANK)
        out[q] = jnp.dot(
            factor, hit.astype(jnp.float32).astype(jnp.bfloat16), preferred_element_type=jnp.float32
        ).astype(jnp.bfloat16)


def spread_out(side):
    return pl.pallas_call(
        spread_kernel,
        out_shape=jax.ShapeDtypeStruct((4, GROUPS * ROWS, 2 * RANK), jnp.bfloat16),
        compiler_params=pltpu.CompilerParams(vmem_limit_bytes=16 * 2**20),
        cost_estimate=pl.CostEstimate(flops=2**26, bytes_accessed=2**20, transcendentals=0),
        name="spread_out",
    )(side)


def grow_kernel(factors, shrunk, mine, theirs):
    count = TOKENS // GROUPS
    values = shrunk[...].astype(jnp.float32)
    low = values[:, 0:8, :].reshape(2 * RANK, LANES).T.astype(jnp.bfloat16)
    high = values[:, 8:16, :].reshape(2 * RANK, LANES).T.astype(jnp.bfloat16)
    half = GROUPS * ROWS
    for q in range(4):
        to = mine if q < 2 else theirs
        columns = pl.ds(q % 2 * half, half)
        to[pl.ds(0, LANES), columns] = lax.dot_general(
            low, factors[q], (((1,), (1,)), ((), ())), preferred_element_type=jnp.float32
        )
        to[pl.ds(LANES, count - LANES), columns] = lax.dot_general(
            high, factors[q], (((1,), (1,)), ((), ())), preferred_element_type=jnp.float32
        )[: count - LANES]


def grow(factors, shrunk):
    shape = jax.ShapeDtypeStruct((TOKENS // GROUPS, 2 * GROUPS * ROWS), jnp.float32)
    return pl.pallas_call(
        grow_kernel,
        out_shape=[shape, shape],
        compiler_params=pltpu.CompilerParams(vmem_limit_bytes=32 * 2**20),
        cost_estimate=pl.CostEstimate(flops=2**25, bytes_accessed=2**20, transcendentals=0),
        name="grow",
    )(factors, shrunk)


def finish_kernel(core, mine, both, out):
    half = GROUPS * ROWS
    other = both.at[1 - core[0]]
    gate = mine[:, :half] + other[:, :half]
    up = mine[:, half:] + other[:, half:]
    out[...] = (gate / (1.0 + jnp.exp(-gate)) * up).astype(jnp.bfloat16)


def finish(core, mine, both):
    vmem = pl.BlockSpec(memory_space=pltpu.VMEM)
    return pl.pallas_call(
        finish_kernel,
        in_specs=[pl.BlockSpec(memory_space=pltpu.SMEM), vmem, vmem],
        out_specs=vmem,
        out_shape=jax.ShapeDtypeStruct((TOKENS // GROUPS, GROUPS * ROWS), jnp.bfloat16),
        compiler_params=pltpu.CompilerParams(vmem_limit_bytes=32 * 2**20),
        cost_estimate=pl.CostEstimate(flops=2**20, bytes_accessed=3 * 2**19, transcendentals=2**16),
        name="finish",
    )(core, mine, both)


def base_term(blocks, other, tokens):
    weights = jnp.concatenate([other[:GROUPS], blocks[:GROUPS]], axis=1)
    weights = lax.all_to_all(weights, TENSOR, 0, 0, tiled=True)
    parts = project(weights, tokens)
    parts = lax.all_to_all(parts.reshape(GROUPS, TOKENS // GROUPS, -1), TENSOR, 0, 0, tiled=True)
    return tuple(add_up(parts))


def adapter_term(blocks, other, tokens):
    side = lax.all_to_all(shrink(blocks, other, tokens), TENSOR, 0, 0, tiled=True)
    copies = copies_of(side, lax.axis_size("xl") * lax.axis_size("z"))
    shrunk = lax.all_to_all(copies, ("xl", "z"), 0, 0, tiled=True)
    return tuple(grow(spread_out(side), shrunk))


def per_device(tokens, gate_ids, up_ids, gate_powers, up_powers, gate_b, up_b, gate_a, up_a):
    core = lax.axis_index("c").astype(jnp.int32)
    blocks = decode(gate_ids, up_ids, gate_powers, up_powers, gate_b, up_b, gate_a, up_a)
    other = lax.ppermute(blocks, "c", [(0, 1), (1, 0)])
    mine, theirs = lax.cond(core == 0, adapter_term, base_term, blocks, other, tokens)
    return finish(core.reshape(1), mine, lax.all_gather(theirs, "c", axis=0))


def solution(mesh):
    split = Mesh(mesh.devices.reshape(2, 16, 2, 4, 2), ("xl", "z", "c", "y", "xh"))
    rows = P(FSDP + TENSOR, None)
    placed = (P(None, TENSOR), rows, rows, rows, rows, rows, rows, P(FSDP, TENSOR), P(FSDP, TENSOR))
    return jax.shard_map(per_device, mesh=split, in_specs=placed, out_specs=P(TENSOR, FSDP), check_vma=False)
```

```python
import jax
import jax.numpy as jnp
import ml_dtypes
from jax import lax
from jax.experimental import pallas as pl
from jax.experimental.pallas import tpu as pltpu
from jax.sharding import Mesh
from jax.sharding import PartitionSpec as P

BLOCK = 64
RANK = 128
GROUPS = 8
ROWS = 32
WIDTH = 1024
TOKENS = 1344
LANES = 128
PAIRS = 4
PIECES = 2
SIDE = 144

NF4_LEVELS = (
    -1.0,
    -0.6961928009986877,
    -0.5250730514526367,
    -0.39491748809814453,
    -0.28444138169288635,
    -0.18477343022823334,
    -0.09105003625154495,
    0.0,
    0.07958029955625534,
    0.16093020141124725,
    0.24611230194568634,
    0.3379152408981323,
    0.44070982933044434,
    0.5626170039176941,
    0.7229568362236023,
    1.0,
)
LEVELS = tuple(float(ml_dtypes.bfloat16(v)) for v in NF4_LEVELS)

FSDP = ("xl", "z", "c")
TENSOR = ("y", "xh")
def pick(ids, low, high):
    if high - low == 1:
        return jnp.full(ids.shape, LEVELS[low], jnp.bfloat16)
    middle = (low + high) // 2
    return jnp.where(ids < jnp.int16(middle), pick(ids, low, middle), pick(ids, middle, high))


def lookup(table, index):
    return jnp.take_along_axis(table, index, axis=1, mode="promise_in_bounds")


def decode_kernel(own, gate_ids, up_ids, gate_powers, up_powers, gate_b, up_b, gate_a, up_a, out, ids, small, thin, blocks, ready, near, sent):
    extra, stores = [], []
    for p, (powers, factor, a) in enumerate(((gate_powers, gate_b, gate_a), (up_powers, up_b, up_a))):
        extra.append(pltpu.make_async_copy(powers, small.at[p], near.at[p]))
        extra.append(pltpu.make_async_copy(a, thin.at[p], near.at[2 + p]))
        place = out.at[PAIRS, pl.ds(p * ROWS, ROWS), pl.ds(0, RANK)]
        stores.append(pltpu.make_async_copy(factor, place, sent.at[PAIRS + 1 + p]))
    loads, groups = [], []
    for k in range(GROUPS):
        group = k // 2 * 2 + (own[0] + k % 2) % 2
        groups.append(group)
        columns = pl.ds(pl.multiple_of(group * WIDTH, WIDTH), WIDTH)
        loads.append(
            [pltpu.make_async_copy(ref.at[:, columns], ids.at[p, k], ready.at[p, k]) for p, ref in enumerate((gate_ids, up_ids))]
        )
    for copy in extra + sum(loads, []) + stores:
        copy.start()
    for copy in extra:
        copy.wait()
    rows = jnp.concatenate([thin[0].astype(jnp.float32), thin[1].astype(jnp.float32), jnp.zeros((12, WIDTH), jnp.float32)], axis=0)
    blocks[PAIRS, pl.ds(0, 16), pl.ds(0, WIDTH)] = rows.astype(jnp.bfloat16)
    stores.append(
        pltpu.make_async_copy(
            blocks.at[PAIRS, pl.ds(0, 16), pl.ds(0, WIDTH)], out.at[PAIRS, pl.ds(0, 16), pl.ds(WIDTH, WIDTH)], sent.at[PAIRS]
        )
    )
    stores[-1].start()
    half = lax.broadcasted_iota(jnp.int32, (ROWS, LANES), 1) // BLOCK
    scales = [(jnp.int32(1) << (small[p] + 8)).astype(jnp.float32) * 2.0**-8 for p in range(2)]
    for k in range(GROUPS):
        for p in range(2):
            loads[k][p].wait()
            rows = pl.ds(p * ROWS, ROWS)
            for chunk in range(WIDTH // LANES):
                level = pick(ids[p, k, :, pl.ds(chunk * LANES, LANES)].astype(jnp.int16), 0, len(LEVELS))
                scale = lookup(scales[p], half + (groups[k] * (WIDTH // BLOCK) + chunk * (LANES // BLOCK)))
                columns = pl.ds(k % 2 * WIDTH + chunk * LANES, LANES)
                blocks[k // 2, rows, columns] = level * scale.astype(jnp.bfloat16)
        if k % 2:
            stores.append(pltpu.make_async_copy(blocks.at[k // 2], out.at[k // 2], sent.at[k // 2]))
            stores[-1].start()
    for store in stores:
        store.wait()


def decode(*args):
    shape = (PAIRS + 1, 2 * ROWS, 2 * WIDTH)
    hbm = pl.BlockSpec(memory_space=pltpu.HBM)
    return pl.pallas_call(
        decode_kernel,
        in_specs=[pl.BlockSpec(memory_space=pltpu.SMEM)] + [hbm] * 8,
        out_specs=hbm,
        out_shape=jax.ShapeDtypeStruct(shape, jnp.bfloat16),
        scratch_shapes=[
            pltpu.VMEM((2, GROUPS, ROWS, WIDTH), jnp.int32),
            pltpu.VMEM((2, ROWS, LANES), jnp.int32),
            pltpu.VMEM((2, 2, WIDTH), jnp.bfloat16),
            pltpu.VMEM(shape, jnp.bfloat16),
            pltpu.SemaphoreType.DMA((2, GROUPS)),
            pltpu.SemaphoreType.DMA((4,)),
            pltpu.SemaphoreType.DMA((PAIRS + 3,)),
        ],
        compiler_params=pltpu.CompilerParams(vmem_limit_bytes=62 * 2**20),
        cost_estimate=pl.CostEstimate(flops=2**24, bytes_accessed=3 * 2**20, transcendentals=0),
        name="decode",
    )(*args)


DIMS = (((1,), (1,)), ((), ()))


def project_own_kernel(weights, tokens, out, rest, merged):
    part = PAIRS * ROWS
    for q in range(4):
        merged[pl.ds(q * part, part), :] = weights[:, pl.ds(q * ROWS, ROWS), pl.ds(0, WIDTH)].reshape(part, WIDTH)
        rest[pl.ds(q * part, part), :] = weights[:, pl.ds(q * ROWS, ROWS), pl.ds(WIDTH, WIDTH)].reshape(part, WIDTH)
    out[...] = lax.dot_general(tokens[...], merged[...], DIMS, preferred_element_type=jnp.float32)


def project_own(weights, tokens):
    place = pl.BlockSpec(memory_space=pltpu.VMEM)
    columns = 4 * PAIRS * ROWS
    return pl.pallas_call(
        project_own_kernel,
        in_specs=[place, place],
        out_specs=[place, place],
        out_shape=[
            jax.ShapeDtypeStruct((TOKENS, columns), jnp.float32),
            jax.ShapeDtypeStruct((columns, WIDTH), jnp.bfloat16),
        ],
        scratch_shapes=[pltpu.VMEM((columns, WIDTH), jnp.bfloat16)],
        compiler_params=pltpu.CompilerParams(vmem_limit_bytes=32 * 2**20),
        cost_estimate=pl.CostEstimate(flops=TOKENS * 1024 * 1024, bytes_accessed=8 * 2**20, transcendentals=0),
        name="project_own",
    )(weights, tokens)


def project_near_kernel(total, weights, tokens, out, held, ready):
    part = TOKENS // PIECES
    loads = []
    for i in range(PIECES):
        rows = pl.ds(i * part, part)
        loads.append(pltpu.make_async_copy(tokens.at[rows], held.at[rows], ready.at[i]))
        loads[-1].start()
    for i in range(PIECES):
        rows = pl.ds(i * part, part)
        loads[i].wait()
        product = lax.dot_general(held[rows, :], weights[...], DIMS, preferred_element_type=jnp.float32)
        out[rows, :] = (total[rows, :] + product).astype(jnp.bfloat16)


def project_near(total, weights, tokens):
    place = pl.BlockSpec(memory_space=pltpu.VMEM)
    return pl.pallas_call(
        project_near_kernel,
        in_specs=[place, place, pl.BlockSpec(memory_space=pltpu.HBM)],
        out_specs=place,
        out_shape=jax.ShapeDtypeStruct(total.shape, jnp.bfloat16),
        scratch_shapes=[pltpu.VMEM((TOKENS, WIDTH), jnp.bfloat16), pltpu.SemaphoreType.DMA((PIECES,))],
        compiler_params=pltpu.CompilerParams(vmem_limit_bytes=32 * 2**20),
        cost_estimate=pl.CostEstimate(flops=TOKENS * 1024 * 1024, bytes_accessed=8 * 2**20, transcendentals=0),
        name="project_near",
    )(total, weights, tokens)


def add_up_kernel(parts, mine, theirs):
    part = PAIRS * ROWS
    for x in range(2):
        total = parts[x].astype(jnp.float32)
        for y in range(1, PAIRS):
            total = total + parts[2 * y + x].astype(jnp.float32)
        for q in range(4):
            to = theirs if q < 2 else mine
            to[:, pl.ds((q % 2 * 2 + x) * part, part)] = total[:, q * part : (q + 1) * part]


def add_up(parts):
    shape = jax.ShapeDtypeStruct((parts.shape[1], parts.shape[2]), jnp.float32)
    return pl.pallas_call(
        add_up_kernel,
        out_shape=[shape, shape],
        compiler_params=pltpu.CompilerParams(vmem_limit_bytes=32 * 2**20),
        cost_estimate=pl.CostEstimate(flops=2**21, bytes_accessed=3 * 2**20, transcendentals=0),
        name="add_up",
    )(parts)


def shrink_kernel(first, second, tokens, out):
    a = [block[0, pl.ds(0, 16), pl.ds(WIDTH, WIDTH)].astype(jnp.float32)[0:4] for block in (first, second)]
    a = jnp.concatenate(a, axis=0).astype(jnp.bfloat16)
    count = TOKENS // GROUPS
    for k in range(GROUPS):
        out[k, pl.ds(0, 2 * ROWS), :] = first[0, :, pl.ds(0, RANK)]
        out[k, pl.ds(2 * ROWS, 2 * ROWS), :] = second[0, :, pl.ds(0, RANK)]
        product = lax.dot_general(a, tokens[k], (((1,), (1,)), ((), ())), preferred_element_type=jnp.float32)
        rest = jnp.concatenate([product[:, LANES:], jnp.zeros((8, 2 * LANES - count), jnp.float32)], axis=1)
        out[k, pl.ds(4 * ROWS, 16), :] = jnp.concatenate([product[:, :LANES], rest], axis=0).astype(jnp.bfloat16)


def shrink(first, second, tokens):
    side = pl.BlockSpec((1, 2 * ROWS, 2 * WIDTH), lambda i: (PAIRS, 0, 0))
    return pl.pallas_call(
        shrink_kernel,
        grid=(1,),
        in_specs=[side, side, pl.BlockSpec((GROUPS, TOKENS // GROUPS, WIDTH), lambda i: (0, 0, 0))],
        out_specs=pl.BlockSpec((GROUPS, SIDE, LANES), lambda i: (0, 0, 0)),
        out_shape=jax.ShapeDtypeStruct((GROUPS, SIDE, LANES), jnp.bfloat16),
        compiler_params=pltpu.CompilerParams(vmem_limit_bytes=40 * 2**20),
        cost_estimate=pl.CostEstimate(flops=2**24, bytes_accessed=3 * 2**20, transcendentals=0),
        name="shrink",
    )(first, second, tokens.reshape(GROUPS, TOKENS // GROUPS, WIDTH))


def copies_kernel(side, out):
    total = side[0, pl.ds(4 * ROWS, 16), :].astype(jnp.float32)
    for k in range(1, GROUPS):
        total = total + side[k, pl.ds(4 * ROWS, 16), :].astype(jnp.float32)
    for place in range(out.shape[0]):
        out[place] = total.astype(jnp.bfloat16)


def copies_of(side, count):
    return pl.pallas_call(
        copies_kernel,
        out_shape=jax.ShapeDtypeStruct((count, 16, LANES), jnp.bfloat16),
        cost_estimate=pl.CostEstimate(flops=2**14, bytes_accessed=2**19, transcendentals=0),
        name="copies",
    )(side)


def spread_kernel(side, out):
    rank = lax.broadcasted_iota(jnp.int32, (RANK, 2 * RANK), 0)
    place = lax.broadcasted_iota(jnp.int32, (RANK, 2 * RANK), 1)
    for q in range(4):
        hit = (place % 4 // 2 == q % 2) & (place // 4 * 2 + place % 2 == rank)
        factor = jnp.concatenate([side[k, pl.ds(q * ROWS, ROWS), :] for k in (0, 2, 4, 6, 1, 3, 5, 7)], axis=0)
        out[q] = jnp.dot(
            factor, hit.astype(jnp.float32).astype(jnp.bfloat16), preferred_element_type=jnp.float32
        ).astype(jnp.bfloat16)


def spread_out(side):
    return pl.pallas_call(
        spread_kernel,
        out_shape=jax.ShapeDtypeStruct((4, GROUPS * ROWS, 2 * RANK), jnp.bfloat16),
        compiler_params=pltpu.CompilerParams(vmem_limit_bytes=16 * 2**20),
        cost_estimate=pl.CostEstimate(flops=2**26, bytes_accessed=2**20, transcendentals=0),
        name="spread_out",
    )(side)


def grow_kernel(factors, shrunk, mine, theirs):
    count = TOKENS // GROUPS
    values = shrunk[...].astype(jnp.float32)
    low = values[:, 0:8, :].reshape(2 * RANK, LANES).T.astype(jnp.bfloat16)
    high = values[:, 8:16, :].reshape(2 * RANK, LANES).T.astype(jnp.bfloat16)
    half = GROUPS * ROWS
    for q in range(4):
        to = mine if q < 2 else theirs
        columns = pl.ds(q % 2 * half, half)
        to[pl.ds(0, LANES), columns] = lax.dot_general(
            low, factors[q], (((1,), (1,)), ((), ())), preferred_element_type=jnp.float32
        )
        to[pl.ds(LANES, count - LANES), columns] = lax.dot_general(
            high, factors[q], (((1,), (1,)), ((), ())), preferred_element_type=jnp.float32
        )[: count - LANES]


def grow(factors, shrunk):
    shape = jax.ShapeDtypeStruct((TOKENS // GROUPS, 2 * GROUPS * ROWS), jnp.float32)
    return pl.pallas_call(
        grow_kernel,
        out_shape=[shape, shape],
        compiler_params=pltpu.CompilerParams(vmem_limit_bytes=32 * 2**20),
        cost_estimate=pl.CostEstimate(flops=2**25, bytes_accessed=2**20, transcendentals=0),
        name="grow",
    )(factors, shrunk)


def finish_kernel(core, mine, both, out):
    half = GROUPS * ROWS
    other = both.at[1 - core[0]]
    gate = mine[:, :half] + other[:, :half]
    up = mine[:, half:] + other[:, half:]
    result = (gate / (1.0 + jnp.exp(-gate)) * up).astype(jnp.bfloat16)
    place = lax.broadcasted_iota(jnp.int32, (half, half), 0)
    column = lax.broadcasted_iota(jnp.int32, (half, half), 1)
    group = column // ROWS
    wanted = (group % 2 * PAIRS + group // 2) * ROWS + column % ROWS
    move = (place == wanted).astype(jnp.float32).astype(jnp.bfloat16)
    out[...] = jnp.dot(result, move, preferred_element_type=jnp.float32).astype(jnp.bfloat16)


def finish(core, mine, both):
    vmem = pl.BlockSpec(memory_space=pltpu.VMEM)
    return pl.pallas_call(
        finish_kernel,
        in_specs=[pl.BlockSpec(memory_space=pltpu.SMEM), vmem, vmem],
        out_specs=vmem,
        out_shape=jax.ShapeDtypeStruct((TOKENS // GROUPS, GROUPS * ROWS), jnp.bfloat16),
        compiler_params=pltpu.CompilerParams(vmem_limit_bytes=32 * 2**20),
        cost_estimate=pl.CostEstimate(flops=2**20, bytes_accessed=3 * 2**19, transcendentals=2**16),
        name="finish",
    )(core, mine, both)


def exchange_weights(blocks, other, tokens):
    weights = jnp.concatenate([other[:PAIRS], blocks[:PAIRS]], axis=1)
    weights = lax.all_to_all(weights, "y", 0, 0, tiled=True)
    return *project_own(weights, tokens), jnp.zeros((GROUPS, SIDE, LANES), jnp.bfloat16)


def exchange_shrunk(blocks, other, tokens):
    side = lax.all_to_all(shrink(blocks, other, tokens), TENSOR, 0, 0, tiled=True)
    columns = 4 * PAIRS * ROWS
    return jnp.zeros((TOKENS, columns), jnp.float32), jnp.zeros((columns, WIDTH), jnp.bfloat16), side


def base_term(total, weights, side, near_tokens):
    parts = project_near(total, weights, near_tokens)
    parts = lax.all_to_all(parts.reshape(GROUPS, TOKENS // GROUPS, -1), TENSOR, 0, 0, tiled=True)
    return tuple(add_up(parts))


def adapter_term(total, weights, side, near_tokens):
    copies = copies_of(side, lax.axis_size("xl") * lax.axis_size("z"))
    shrunk = lax.all_to_all(copies, ("xl", "z"), 0, 0, tiled=True)
    return tuple(grow(spread_out(side), shrunk))


def per_device(tokens, gate_ids, up_ids, gate_powers, up_powers, gate_b, up_b, gate_a, up_a):
    core = lax.axis_index("c").astype(jnp.int32)
    pairs = [(xl * 4 + 2 + xh, (1 - xl) * 4 + 2 + 1 - xh) for xl in range(2) for xh in range(2)]
    near_tokens = lax.ppermute(tokens, ("xl", "c", "xh"), pairs)
    own = lax.axis_index("xh").astype(jnp.int32).reshape(1)
    blocks = decode(own, gate_ids, up_ids, gate_powers, up_powers, gate_b, up_b, gate_a, up_a)
    other = lax.ppermute(blocks, "c", [(0, 1), (1, 0)])
    total, weights, side = lax.cond(core == 0, exchange_shrunk, exchange_weights, blocks, other, tokens)
    mine, theirs = lax.cond(core == 0, adapter_term, base_term, total, weights, side, near_tokens)
    return finish(core.reshape(1), mine, lax.all_gather(theirs, "c", axis=0))


def solution(mesh):
    split = Mesh(mesh.devices.reshape(2, 16, 2, 4, 2), ("xl", "z", "c", "y", "xh"))
    rows = P(FSDP + TENSOR, None)
    placed = (P(None, TENSOR), rows, rows, rows, rows, rows, rows, P(FSDP, TENSOR), P(FSDP, TENSOR))
    return jax.shard_map(per_device, mesh=split, in_specs=placed, out_specs=P(TENSOR, FSDP), check_vma=False)
```

```python
import jax
import jax.numpy as jnp
import ml_dtypes
from jax import lax
from jax.experimental import pallas as pl
from jax.experimental.pallas import tpu as pltpu
from jax.sharding import Mesh
from jax.sharding import PartitionSpec as P

BLOCK = 64
RANK = 128
GROUPS = 8
ROWS = 32
WIDTH = 1024
TOKENS = 1344
LANES = 128
PAIRS = 4
PIECES = 2
HELD = 2 * 4 * 32
SIDE = 144

NF4_LEVELS = (
    -1.0,
    -0.6961928009986877,
    -0.5250730514526367,
    -0.39491748809814453,
    -0.28444138169288635,
    -0.18477343022823334,
    -0.09105003625154495,
    0.0,
    0.07958029955625534,
    0.16093020141124725,
    0.24611230194568634,
    0.3379152408981323,
    0.44070982933044434,
    0.5626170039176941,
    0.7229568362236023,
    1.0,
)
LEVELS = tuple(float(ml_dtypes.bfloat16(v)) for v in NF4_LEVELS)

FSDP = ("xl", "z", "c")
TENSOR = ("y", "xh")
def pick(ids, low, high):
    if high - low == 1:
        return jnp.full(ids.shape, LEVELS[low], jnp.bfloat16)
    middle = (low + high) // 2
    return jnp.where(ids < jnp.int16(middle), pick(ids, low, middle), pick(ids, middle, high))


def lookup(table, index):
    return jnp.take_along_axis(table, index, axis=1, mode="promise_in_bounds")


def decode_kernel(own, gate_ids, up_ids, gate_powers, up_powers, gate_b, up_b, gate_a, up_a, out, ids, small, thin, blocks, ready, near, sent):
    extra, stores = [], []
    for p, (powers, factor, a) in enumerate(((gate_powers, gate_b, gate_a), (up_powers, up_b, up_a))):
        extra.append(pltpu.make_async_copy(powers, small.at[p], near.at[p]))
        extra.append(pltpu.make_async_copy(a, thin.at[p], near.at[2 + p]))
        for h in range(2):
            place = out.at[pl.ds(HELD, 16), pl.ds((2 * p + h) * RANK, RANK)]
            stores.append(pltpu.make_async_copy(factor.at[pl.ds(h * 16, 16)], place, sent.at[PAIRS + 1 + 2 * p + h]))
    loads, groups = [], []
    for k in range(GROUPS):
        group = k // 2 * 2 + (own[0] + k % 2) % 2
        groups.append(group)
        columns = pl.ds(pl.multiple_of(group * WIDTH, WIDTH), WIDTH)
        loads.append(
            [pltpu.make_async_copy(ref.at[:, columns], ids.at[p, k], ready.at[p, k]) for p, ref in enumerate((gate_ids, up_ids))]
        )
    for copy in extra + sum(loads, []) + stores:
        copy.start()
    for copy in extra:
        copy.wait()
    rows = jnp.concatenate([thin[0].astype(jnp.float32), thin[1].astype(jnp.float32), jnp.zeros((12, WIDTH), jnp.float32)], axis=0)
    blocks[pl.ds(HELD, 16), pl.ds(WIDTH, WIDTH)] = rows.astype(jnp.bfloat16)
    last = (pl.ds(HELD, 16), pl.ds(WIDTH, WIDTH))
    stores.append(pltpu.make_async_copy(blocks.at[last], out.at[last], sent.at[PAIRS]))
    stores[-1].start()
    half = lax.broadcasted_iota(jnp.int32, (ROWS, LANES), 1) // BLOCK
    scales = [(jnp.int32(1) << (small[p] + 8)).astype(jnp.float32) * 2.0**-8 for p in range(2)]
    for k in range(GROUPS):
        for p in range(2):
            loads[k][p].wait()
            rows = pl.ds(k // 2 * 2 * ROWS + p * ROWS, ROWS)
            for chunk in range(WIDTH // LANES):
                level = pick(ids[p, k, :, pl.ds(chunk * LANES, LANES)].astype(jnp.int16), 0, len(LEVELS))
                scale = lookup(scales[p], half + (groups[k] * (WIDTH // BLOCK) + chunk * (LANES // BLOCK)))
                columns = pl.ds(k % 2 * WIDTH + chunk * LANES, LANES)
                blocks[rows, columns] = level * scale.astype(jnp.bfloat16)
        if k % 2:
            rows = pl.ds(k // 2 * 2 * ROWS, 2 * ROWS)
            stores.append(pltpu.make_async_copy(blocks.at[rows], out.at[rows], sent.at[k // 2]))
            stores[-1].start()
    for store in stores:
        store.wait()


def decode(*args):
    shape = (HELD + 16, 2 * WIDTH)
    hbm = pl.BlockSpec(memory_space=pltpu.HBM)
    return pl.pallas_call(
        decode_kernel,
        in_specs=[pl.BlockSpec(memory_space=pltpu.SMEM)] + [hbm] * 8,
        out_specs=hbm,
        out_shape=jax.ShapeDtypeStruct(shape, jnp.bfloat16),
        scratch_shapes=[
            pltpu.VMEM((2, GROUPS, ROWS, WIDTH), jnp.int32),
            pltpu.VMEM((2, ROWS, LANES), jnp.int32),
            pltpu.VMEM((2, 2, WIDTH), jnp.bfloat16),
            pltpu.VMEM(shape, jnp.bfloat16),
            pltpu.SemaphoreType.DMA((2, GROUPS)),
            pltpu.SemaphoreType.DMA((4,)),
            pltpu.SemaphoreType.DMA((PAIRS + 5,)),
        ],
        compiler_params=pltpu.CompilerParams(vmem_limit_bytes=62 * 2**20),
        cost_estimate=pl.CostEstimate(flops=2**24, bytes_accessed=3 * 2**20, transcendentals=0),
        name="decode",
    )(*args)


DIMS = (((1,), (1,)), ((), ()))


def project_own_kernel(weights, tokens, out, rest, merged):
    part = PAIRS * ROWS
    for q in range(4):
        merged[pl.ds(q * part, part), :] = weights[:, pl.ds(q * ROWS, ROWS), pl.ds(0, WIDTH)].reshape(part, WIDTH)
        rest[pl.ds(q * part, part), :] = weights[:, pl.ds(q * ROWS, ROWS), pl.ds(WIDTH, WIDTH)].reshape(part, WIDTH)
    out[...] = lax.dot_general(tokens[...], merged[...], DIMS, preferred_element_type=jnp.float32)


def project_own(weights, tokens):
    place = pl.BlockSpec(memory_space=pltpu.VMEM)
    columns = 4 * PAIRS * ROWS
    return pl.pallas_call(
        project_own_kernel,
        in_specs=[place, place],
        out_specs=[place, place],
        out_shape=[
            jax.ShapeDtypeStruct((TOKENS, columns), jnp.float32),
            jax.ShapeDtypeStruct((columns, WIDTH), jnp.bfloat16),
        ],
        scratch_shapes=[pltpu.VMEM((columns, WIDTH), jnp.bfloat16)],
        compiler_params=pltpu.CompilerParams(vmem_limit_bytes=32 * 2**20),
        cost_estimate=pl.CostEstimate(flops=TOKENS * 1024 * 1024, bytes_accessed=8 * 2**20, transcendentals=0),
        name="project_own",
    )(weights, tokens)


def project_near_kernel(total, weights, tokens, out, held, ready):
    part = TOKENS // PIECES
    loads = []
    for i in range(PIECES):
        rows = pl.ds(i * part, part)
        loads.append(pltpu.make_async_copy(tokens.at[rows], held.at[rows], ready.at[i]))
        loads[-1].start()
    for i in range(PIECES):
        rows = pl.ds(i * part, part)
        loads[i].wait()
        product = lax.dot_general(held[rows, :], weights[...], DIMS, preferred_element_type=jnp.float32)
        out[rows, :] = (total[rows, :] + product).astype(jnp.bfloat16)


def project_near(total, weights, tokens):
    place = pl.BlockSpec(memory_space=pltpu.VMEM)
    return pl.pallas_call(
        project_near_kernel,
        in_specs=[place, place, pl.BlockSpec(memory_space=pltpu.HBM)],
        out_specs=place,
        out_shape=jax.ShapeDtypeStruct(total.shape, jnp.bfloat16),
        scratch_shapes=[pltpu.VMEM((TOKENS, WIDTH), jnp.bfloat16), pltpu.SemaphoreType.DMA((PIECES,))],
        compiler_params=pltpu.CompilerParams(vmem_limit_bytes=32 * 2**20),
        cost_estimate=pl.CostEstimate(flops=TOKENS * 1024 * 1024, bytes_accessed=8 * 2**20, transcendentals=0),
        name="project_near",
    )(total, weights, tokens)


def add_up_kernel(parts, mine, theirs):
    part = PAIRS * ROWS
    for x in range(2):
        total = parts[x].astype(jnp.float32)
        for y in range(1, PAIRS):
            total = total + parts[2 * y + x].astype(jnp.float32)
        for q in range(4):
            to = theirs if q < 2 else mine
            to[:, pl.ds((q % 2 * 2 + x) * part, part)] = total[:, q * part : (q + 1) * part]


def add_up(parts):
    shape = jax.ShapeDtypeStruct((parts.shape[1], parts.shape[2]), jnp.float32)
    return pl.pallas_call(
        add_up_kernel,
        out_shape=[shape, shape],
        compiler_params=pltpu.CompilerParams(vmem_limit_bytes=32 * 2**20),
        cost_estimate=pl.CostEstimate(flops=2**21, bytes_accessed=3 * 2**20, transcendentals=0),
        name="add_up",
    )(parts)


def shrink_kernel(first, second, tokens, out, *rest):
    a = [block[:, pl.ds(WIDTH, WIDTH)].astype(jnp.float32)[0:4] for block in (first, second)]
    a = jnp.concatenate(a, axis=0).astype(jnp.bfloat16)
    count = TOKENS // GROUPS
    step = pl.program_id(0) * tokens.shape[0]
    for k in range(tokens.shape[0]):
        for c, block in enumerate((first, second)):
            for h in range(4):
                out[step + k, pl.ds(c * 2 * ROWS + h * 16, 16), :] = block[:, pl.ds(h * RANK, RANK)]
        product = lax.dot_general(a, tokens[k], (((1,), (1,)), ((), ())), preferred_element_type=jnp.float32)
        high = jnp.concatenate([product[:, LANES:], jnp.zeros((8, 2 * LANES - count), jnp.float32)], axis=1)
        both = jnp.concatenate([product[:, :LANES], high], axis=0)
        out[step + k, pl.ds(4 * ROWS, 16), :] = both.astype(jnp.bfloat16)


def shrink(first, second, tokens, steps=2):
    side = pl.BlockSpec((16, 2 * WIDTH), lambda i: (HELD // 16, 0))
    columns = 4 * PAIRS * ROWS
    room = pl.BlockSpec(memory_space=pl.ANY)
    return pl.pallas_call(
        shrink_kernel,
        grid=(steps,),
        in_specs=[side, side, pl.BlockSpec((GROUPS // steps, TOKENS // GROUPS, WIDTH), lambda i: (i, 0, 0))],
        out_specs=[pl.BlockSpec((GROUPS, SIDE, LANES), lambda i: (0, 0, 0)), room, room],
        out_shape=[
            jax.ShapeDtypeStruct((GROUPS, SIDE, LANES), jnp.bfloat16),
            jax.ShapeDtypeStruct((TOKENS, columns), jnp.float32),
            jax.ShapeDtypeStruct((columns, WIDTH), jnp.bfloat16),
        ],
        compiler_params=pltpu.CompilerParams(vmem_limit_bytes=40 * 2**20),
        cost_estimate=pl.CostEstimate(flops=2**24, bytes_accessed=3 * 2**20, transcendentals=0),
        name="shrink",
    )(first, second, tokens.reshape(GROUPS, TOKENS // GROUPS, WIDTH))


def copies_kernel(side, out):
    total = side[0, pl.ds(4 * ROWS, 16), :].astype(jnp.float32)
    for k in range(1, GROUPS):
        total = total + side[k, pl.ds(4 * ROWS, 16), :].astype(jnp.float32)
    for place in range(out.shape[0]):
        out[place] = total.astype(jnp.bfloat16)


def copies_of(side, count):
    return pl.pallas_call(
        copies_kernel,
        out_shape=jax.ShapeDtypeStruct((count, 16, LANES), jnp.bfloat16),
        cost_estimate=pl.CostEstimate(flops=2**14, bytes_accessed=2**19, transcendentals=0),
        name="copies",
    )(side)


def spread_kernel(side, out):
    rank = lax.broadcasted_iota(jnp.int32, (RANK, 2 * RANK), 0)
    place = lax.broadcasted_iota(jnp.int32, (RANK, 2 * RANK), 1)
    for q in range(4):
        hit = (place % 4 // 2 == q % 2) & (place // 4 * 2 + place % 2 == rank)
        factor = jnp.concatenate([side[k, pl.ds(q * ROWS, ROWS), :] for k in (0, 2, 4, 6, 1, 3, 5, 7)], axis=0)
        out[q] = jnp.dot(
            factor, hit.astype(jnp.float32).astype(jnp.bfloat16), preferred_element_type=jnp.float32
        ).astype(jnp.bfloat16)


def spread_out(side):
    return pl.pallas_call(
        spread_kernel,
        out_shape=jax.ShapeDtypeStruct((4, GROUPS * ROWS, 2 * RANK), jnp.bfloat16),
        compiler_params=pltpu.CompilerParams(vmem_limit_bytes=16 * 2**20),
        cost_estimate=pl.CostEstimate(flops=2**26, bytes_accessed=2**20, transcendentals=0),
        name="spread_out",
    )(side)


def grow_kernel(factors, shrunk, mine, theirs):
    count = TOKENS // GROUPS
    values = shrunk[...].astype(jnp.float32)
    low = values[:, 0:8, :].reshape(2 * RANK, LANES).T.astype(jnp.bfloat16)
    high = values[:, 8:16, :].reshape(2 * RANK, LANES).T.astype(jnp.bfloat16)
    half = GROUPS * ROWS
    for q in range(4):
        to = mine if q < 2 else theirs
        columns = pl.ds(q % 2 * half, half)
        to[pl.ds(0, LANES), columns] = lax.dot_general(
            low, factors[q], (((1,), (1,)), ((), ())), preferred_element_type=jnp.float32
        )
        to[pl.ds(LANES, count - LANES), columns] = lax.dot_general(
            high, factors[q], (((1,), (1,)), ((), ())), preferred_element_type=jnp.float32
        )[: count - LANES]


def grow(factors, shrunk):
    shape = jax.ShapeDtypeStruct((TOKENS // GROUPS, 2 * GROUPS * ROWS), jnp.float32)
    return pl.pallas_call(
        grow_kernel,
        out_shape=[shape, shape],
        compiler_params=pltpu.CompilerParams(vmem_limit_bytes=32 * 2**20),
        cost_estimate=pl.CostEstimate(flops=2**25, bytes_accessed=2**20, transcendentals=0),
        name="grow",
    )(factors, shrunk)


def finish_kernel(core, mine, both, out):
    half = GROUPS * ROWS
    other = both.at[1 - core[0]]
    gate = mine[:, :half] + other[:, :half]
    up = mine[:, half:] + other[:, half:]
    result = (gate / (1.0 + jnp.exp(-gate)) * up).astype(jnp.bfloat16)
    place = lax.broadcasted_iota(jnp.int32, (half, half), 0)
    column = lax.broadcasted_iota(jnp.int32, (half, half), 1)
    group = column // ROWS
    wanted = (group % 2 * PAIRS + group // 2) * ROWS + column % ROWS
    move = (place == wanted).astype(jnp.float32).astype(jnp.bfloat16)
    out[...] = jnp.dot(result, move, preferred_element_type=jnp.float32).astype(jnp.bfloat16)


def finish(core, mine, both):
    vmem = pl.BlockSpec(memory_space=pltpu.VMEM)
    return pl.pallas_call(
        finish_kernel,
        in_specs=[pl.BlockSpec(memory_space=pltpu.SMEM), vmem, vmem],
        out_specs=vmem,
        out_shape=jax.ShapeDtypeStruct((TOKENS // GROUPS, GROUPS * ROWS), jnp.bfloat16),
        compiler_params=pltpu.CompilerParams(vmem_limit_bytes=32 * 2**20),
        cost_estimate=pl.CostEstimate(flops=2**20, bytes_accessed=3 * 2**19, transcendentals=2**16),
        name="finish",
    )(core, mine, both)


def exchange_weights(blocks, other, tokens):
    weights = jnp.concatenate([part[:HELD].reshape(PAIRS, 2 * ROWS, 2 * WIDTH) for part in (other, blocks)], axis=1)
    weights = lax.all_to_all(weights, "y", 0, 0, tiled=True)
    return *project_own(weights, tokens), jnp.zeros((GROUPS, SIDE, LANES), jnp.bfloat16)


def exchange_shrunk(blocks, other, tokens):
    side, total, weights = shrink(blocks, other, tokens)
    return total, weights, lax.all_to_all(side, TENSOR, 0, 0, tiled=True)


def base_term(total, weights, side, near_tokens):
    parts = project_near(total, weights, near_tokens)
    parts = lax.all_to_all(parts.reshape(GROUPS, TOKENS // GROUPS, -1), TENSOR, 0, 0, tiled=True)
    return tuple(add_up(parts))


def adapter_term(total, weights, side, near_tokens):
    copies = copies_of(side, lax.axis_size("xl") * lax.axis_size("z"))
    shrunk = lax.all_to_all(copies, ("xl", "z"), 0, 0, tiled=True)
    return tuple(grow(spread_out(side), shrunk))


def per_device(tokens, gate_ids, up_ids, gate_powers, up_powers, gate_b, up_b, gate_a, up_a):
    core = lax.axis_index("c").astype(jnp.int32)
    pairs = [(xl * 4 + 2 + xh, (1 - xl) * 4 + 2 + 1 - xh) for xl in range(2) for xh in range(2)]
    near_tokens = lax.ppermute(tokens, ("xl", "c", "xh"), pairs)
    own = lax.axis_index("xh").astype(jnp.int32).reshape(1)
    blocks = decode(own, gate_ids, up_ids, gate_powers, up_powers, gate_b, up_b, gate_a, up_a)
    other = lax.ppermute(blocks, "c", [(0, 1), (1, 0)])
    total, weights, side = lax.cond(core == 0, exchange_shrunk, exchange_weights, blocks, other, tokens)
    mine, theirs = lax.cond(core == 0, adapter_term, base_term, total, weights, side, near_tokens)
    return finish(core.reshape(1), mine, lax.all_gather(theirs, "c", axis=0))


def solution(mesh):
    split = Mesh(mesh.devices.reshape(2, 16, 2, 4, 2), ("xl", "z", "c", "y", "xh"))
    rows = P(FSDP + TENSOR, None)
    placed = (P(None, TENSOR), rows, rows, rows, rows, rows, rows, P(FSDP, TENSOR), P(FSDP, TENSOR))
    return jax.shard_map(per_device, mesh=split, in_specs=placed, out_specs=P(TENSOR, FSDP), check_vma=False)
```

```python
import jax
import jax.numpy as jnp
import ml_dtypes
from jax import lax
from jax.experimental import pallas as pl
from jax.experimental.pallas import tpu as pltpu
from jax.sharding import Mesh
from jax.sharding import PartitionSpec as P

BLOCK = 64
RANK = 128
GROUPS = 8
ROWS = 32
WIDTH = 1024
TOKENS = 1344
LANES = 128
PAIRS = 4
PIECES = 2
HELD = 2 * 4 * 32
SIDE = 144

NF4_LEVELS = (
    -1.0,
    -0.6961928009986877,
    -0.5250730514526367,
    -0.39491748809814453,
    -0.28444138169288635,
    -0.18477343022823334,
    -0.09105003625154495,
    0.0,
    0.07958029955625534,
    0.16093020141124725,
    0.24611230194568634,
    0.3379152408981323,
    0.44070982933044434,
    0.5626170039176941,
    0.7229568362236023,
    1.0,
)
LEVELS = tuple(float(ml_dtypes.bfloat16(v)) for v in NF4_LEVELS)

FSDP = ("xl", "z", "c")
TENSOR = ("y", "xh")
def pick(ids, low, high):
    if high - low == 1:
        return jnp.full(ids.shape, LEVELS[low], jnp.bfloat16)
    middle = (low + high) // 2
    return jnp.where(ids < jnp.int16(middle), pick(ids, low, middle), pick(ids, middle, high))


def lookup(table, index):
    return jnp.take_along_axis(table, index, axis=1, mode="promise_in_bounds")


def decode_kernel(own, gate_ids, up_ids, gate_powers, up_powers, gate_b, up_b, gate_a, up_a, out, ids, small, thin, blocks, ready, near, sent):
    extra, stores = [], []
    for p, (powers, factor, a) in enumerate(((gate_powers, gate_b, gate_a), (up_powers, up_b, up_a))):
        extra.append(pltpu.make_async_copy(powers, small.at[p], near.at[p]))
        extra.append(pltpu.make_async_copy(a, thin.at[p], near.at[2 + p]))
        for h in range(2):
            place = out.at[pl.ds(HELD, 16), pl.ds((2 * p + h) * RANK, RANK)]
            stores.append(pltpu.make_async_copy(factor.at[pl.ds(h * 16, 16)], place, sent.at[PAIRS + 1 + 2 * p + h]))
    loads, groups = [], []
    for k in range(GROUPS):
        group = k // 2 * 2 + (own[0] + k % 2) % 2
        groups.append(group)
        columns = pl.ds(pl.multiple_of(group * WIDTH, WIDTH), WIDTH)
        loads.append(
            [pltpu.make_async_copy(ref.at[:, columns], ids.at[p, k], ready.at[p, k]) for p, ref in enumerate((gate_ids, up_ids))]
        )
    for copy in extra + sum(loads, []) + stores:
        copy.start()
    for copy in extra:
        copy.wait()
    rows = jnp.concatenate([thin[0].astype(jnp.float32), thin[1].astype(jnp.float32), jnp.zeros((12, WIDTH), jnp.float32)], axis=0)
    blocks[pl.ds(HELD, 16), pl.ds(WIDTH, WIDTH)] = rows.astype(jnp.bfloat16)
    last = (pl.ds(HELD, 16), pl.ds(WIDTH, WIDTH))
    stores.append(pltpu.make_async_copy(blocks.at[last], out.at[last], sent.at[PAIRS]))
    stores[-1].start()
    half = lax.broadcasted_iota(jnp.int32, (ROWS, LANES), 1) // BLOCK
    scales = [(jnp.int32(1) << (small[p] + 8)).astype(jnp.float32) * 2.0**-8 for p in range(2)]
    for k in range(GROUPS):
        for p in range(2):
            loads[k][p].wait()
            rows = pl.ds(k // 2 * 2 * ROWS + p * ROWS, ROWS)
            for chunk in range(WIDTH // LANES):
                level = pick(ids[p, k, :, pl.ds(chunk * LANES, LANES)].astype(jnp.int16), 0, len(LEVELS))
                scale = lookup(scales[p], half + (groups[k] * (WIDTH // BLOCK) + chunk * (LANES // BLOCK)))
                columns = pl.ds(k % 2 * WIDTH + chunk * LANES, LANES)
                blocks[rows, columns] = level * scale.astype(jnp.bfloat16)
        if k % 2:
            rows = pl.ds(k // 2 * 2 * ROWS, 2 * ROWS)
            stores.append(pltpu.make_async_copy(blocks.at[rows], out.at[rows], sent.at[k // 2]))
            stores[-1].start()
    for store in stores:
        store.wait()


def decode(*args):
    shape = (HELD + 16, 2 * WIDTH)
    hbm = pl.BlockSpec(memory_space=pltpu.HBM)
    return pl.pallas_call(
        decode_kernel,
        in_specs=[pl.BlockSpec(memory_space=pltpu.SMEM)] + [hbm] * 8,
        out_specs=hbm,
        out_shape=jax.ShapeDtypeStruct(shape, jnp.bfloat16),
        scratch_shapes=[
            pltpu.VMEM((2, GROUPS, ROWS, WIDTH), jnp.int32),
            pltpu.VMEM((2, ROWS, LANES), jnp.int32),
            pltpu.VMEM((2, 2, WIDTH), jnp.bfloat16),
            pltpu.VMEM(shape, jnp.bfloat16),
            pltpu.SemaphoreType.DMA((2, GROUPS)),
            pltpu.SemaphoreType.DMA((4,)),
            pltpu.SemaphoreType.DMA((PAIRS + 5,)),
        ],
        compiler_params=pltpu.CompilerParams(vmem_limit_bytes=62 * 2**20),
        cost_estimate=pl.CostEstimate(flops=2**24, bytes_accessed=3 * 2**20, transcendentals=0),
        name="decode",
    )(*args)


DIMS = (((1,), (1,)), ((), ()))


def project_own_kernel(weights, tokens, out, rest, merged):
    part = PAIRS * ROWS
    for q in range(4):
        merged[pl.ds(q * part, part), :] = weights[:, pl.ds(q * ROWS, ROWS), pl.ds(0, WIDTH)].reshape(part, WIDTH)
        rest[pl.ds(q * part, part), :] = weights[:, pl.ds(q * ROWS, ROWS), pl.ds(WIDTH, WIDTH)].reshape(part, WIDTH)
    out[...] = lax.dot_general(tokens[...], merged[...], DIMS, preferred_element_type=jnp.float32)


def project_own(weights, tokens):
    place = pl.BlockSpec(memory_space=pltpu.VMEM)
    columns = 4 * PAIRS * ROWS
    return pl.pallas_call(
        project_own_kernel,
        in_specs=[place, place],
        out_specs=[place, place],
        out_shape=[
            jax.ShapeDtypeStruct((TOKENS, columns), jnp.float32),
            jax.ShapeDtypeStruct((columns, WIDTH), jnp.bfloat16),
        ],
        scratch_shapes=[pltpu.VMEM((columns, WIDTH), jnp.bfloat16)],
        compiler_params=pltpu.CompilerParams(vmem_limit_bytes=32 * 2**20),
        cost_estimate=pl.CostEstimate(flops=TOKENS * 1024 * 1024, bytes_accessed=8 * 2**20, transcendentals=0),
        name="project_own",
    )(weights, tokens)


def project_near_kernel(total, weights, tokens, out, held, ready):
    part = TOKENS // PIECES
    loads = []
    for i in range(PIECES):
        rows = pl.ds(i * part, part)
        loads.append(pltpu.make_async_copy(tokens.at[rows], held.at[rows], ready.at[i]))
        loads[-1].start()
    for i in range(PIECES):
        rows = pl.ds(i * part, part)
        loads[i].wait()
        product = lax.dot_general(held[rows, :], weights[...], DIMS, preferred_element_type=jnp.float32)
        out[rows, :] = (total[rows, :] + product).astype(jnp.bfloat16)


def project_near(total, weights, tokens):
    place = pl.BlockSpec(memory_space=pltpu.VMEM)
    return pl.pallas_call(
        project_near_kernel,
        in_specs=[place, place, pl.BlockSpec(memory_space=pltpu.HBM)],
        out_specs=place,
        out_shape=jax.ShapeDtypeStruct(total.shape, jnp.bfloat16),
        scratch_shapes=[pltpu.VMEM((TOKENS, WIDTH), jnp.bfloat16), pltpu.SemaphoreType.DMA((PIECES,))],
        compiler_params=pltpu.CompilerParams(vmem_limit_bytes=32 * 2**20),
        cost_estimate=pl.CostEstimate(flops=TOKENS * 1024 * 1024, bytes_accessed=8 * 2**20, transcendentals=0),
        name="project_near",
    )(total, weights, tokens)


def add_up_kernel(parts, mine, theirs):
    part = PAIRS * ROWS
    for x in range(2):
        total = parts[x].astype(jnp.float32)
        for y in range(1, PAIRS):
            total = total + parts[2 * y + x].astype(jnp.float32)
        for q in range(4):
            to = theirs if q < 2 else mine
            to[:, pl.ds((q % 2 * 2 + x) * part, part)] = total[:, q * part : (q + 1) * part].astype(to.dtype)


def add_up(parts):
    shape = (parts.shape[1], parts.shape[2])
    return pl.pallas_call(
        add_up_kernel,
        out_shape=[jax.ShapeDtypeStruct(shape, jnp.float32), jax.ShapeDtypeStruct(shape, jnp.bfloat16)],
        compiler_params=pltpu.CompilerParams(vmem_limit_bytes=32 * 2**20),
        cost_estimate=pl.CostEstimate(flops=2**21, bytes_accessed=3 * 2**20, transcendentals=0),
        name="add_up",
    )(parts)


def shrink_kernel(first, second, tokens, out, *rest):
    a = [block[:, pl.ds(WIDTH, WIDTH)].astype(jnp.float32)[0:4] for block in (first, second)]
    a = jnp.concatenate(a, axis=0).astype(jnp.bfloat16)
    count = TOKENS // GROUPS
    step = pl.program_id(0) * tokens.shape[0]
    for k in range(tokens.shape[0]):
        for c, block in enumerate((first, second)):
            for h in range(4):
                out[step + k, pl.ds(c * 2 * ROWS + h * 16, 16), :] = block[:, pl.ds(h * RANK, RANK)]
        product = lax.dot_general(a, tokens[k], (((1,), (1,)), ((), ())), preferred_element_type=jnp.float32)
        high = jnp.concatenate([product[:, LANES:], jnp.zeros((8, 2 * LANES - count), jnp.float32)], axis=1)
        both = jnp.concatenate([product[:, :LANES], high], axis=0)
        out[step + k, pl.ds(4 * ROWS, 16), :] = both.astype(jnp.bfloat16)


def shrink(first, second, tokens, steps=2):
    side = pl.BlockSpec((16, 2 * WIDTH), lambda i: (HELD // 16, 0))
    columns = 4 * PAIRS * ROWS
    room = pl.BlockSpec(memory_space=pl.ANY)
    return pl.pallas_call(
        shrink_kernel,
        grid=(steps,),
        in_specs=[side, side, pl.BlockSpec((GROUPS // steps, TOKENS // GROUPS, WIDTH), lambda i: (i, 0, 0))],
        out_specs=[pl.BlockSpec((GROUPS, SIDE, LANES), lambda i: (0, 0, 0)), room, room],
        out_shape=[
            jax.ShapeDtypeStruct((GROUPS, SIDE, LANES), jnp.bfloat16),
            jax.ShapeDtypeStruct((TOKENS, columns), jnp.float32),
            jax.ShapeDtypeStruct((columns, WIDTH), jnp.bfloat16),
        ],
        compiler_params=pltpu.CompilerParams(vmem_limit_bytes=40 * 2**20),
        cost_estimate=pl.CostEstimate(flops=2**24, bytes_accessed=3 * 2**20, transcendentals=0),
        name="shrink",
    )(first, second, tokens.reshape(GROUPS, TOKENS // GROUPS, WIDTH))


def copies_kernel(side, out):
    total = side[0, pl.ds(4 * ROWS, 16), :].astype(jnp.float32)
    for k in range(1, GROUPS):
        total = total + side[k, pl.ds(4 * ROWS, 16), :].astype(jnp.float32)
    for place in range(out.shape[0]):
        out[place] = total.astype(jnp.bfloat16)


def copies_of(side, count):
    return pl.pallas_call(
        copies_kernel,
        out_shape=jax.ShapeDtypeStruct((count, 16, LANES), jnp.bfloat16),
        cost_estimate=pl.CostEstimate(flops=2**14, bytes_accessed=2**19, transcendentals=0),
        name="copies",
    )(side)


def spread_kernel(side, out):
    rank = lax.broadcasted_iota(jnp.int32, (RANK, 2 * RANK), 0)
    place = lax.broadcasted_iota(jnp.int32, (RANK, 2 * RANK), 1)
    slot = place // 4
    owner = slot // 2 % 2 * 32 + slot // 4 * 2 + slot % 2
    for q in range(4):
        hit = (place % 4 // 2 == q % 2) & (owner * 2 + place % 2 == rank)
        factor = jnp.concatenate([side[k, pl.ds(q * ROWS, ROWS), :] for k in (0, 2, 4, 6, 1, 3, 5, 7)], axis=0)
        out[q] = jnp.dot(
            factor, hit.astype(jnp.float32).astype(jnp.bfloat16), preferred_element_type=jnp.float32
        ).astype(jnp.bfloat16)


def spread_out(side):
    return pl.pallas_call(
        spread_kernel,
        out_shape=jax.ShapeDtypeStruct((4, GROUPS * ROWS, 2 * RANK), jnp.bfloat16),
        compiler_params=pltpu.CompilerParams(vmem_limit_bytes=16 * 2**20),
        cost_estimate=pl.CostEstimate(flops=2**26, bytes_accessed=2**20, transcendentals=0),
        name="spread_out",
    )(side)


def grow_kernel(factors, shrunk, mine, theirs):
    count = TOKENS // GROUPS
    values = shrunk[...].astype(jnp.float32)
    low = values[:, 0:8, :].reshape(2 * RANK, LANES).T.astype(jnp.bfloat16)
    high = values[:, 8:16, :].reshape(2 * RANK, LANES).T.astype(jnp.bfloat16)
    half = GROUPS * ROWS
    for q in range(4):
        to = mine if q < 2 else theirs
        columns = pl.ds(q % 2 * half, half)
        to[pl.ds(0, LANES), columns] = lax.dot_general(
            low, factors[q], (((1,), (1,)), ((), ())), preferred_element_type=jnp.float32
        ).astype(to.dtype)
        to[pl.ds(LANES, count - LANES), columns] = lax.dot_general(
            high, factors[q], (((1,), (1,)), ((), ())), preferred_element_type=jnp.float32
        )[: count - LANES].astype(to.dtype)


def grow(factors, shrunk):
    shape = (TOKENS // GROUPS, 2 * GROUPS * ROWS)
    return pl.pallas_call(
        grow_kernel,
        out_shape=[jax.ShapeDtypeStruct(shape, jnp.float32), jax.ShapeDtypeStruct(shape, jnp.bfloat16)],
        compiler_params=pltpu.CompilerParams(vmem_limit_bytes=32 * 2**20),
        cost_estimate=pl.CostEstimate(flops=2**25, bytes_accessed=2**20, transcendentals=0),
        name="grow",
    )(factors, shrunk)


def finish_kernel(core, mine, both, out):
    half = GROUPS * ROWS
    other = both.at[1 - core[0]]
    gate = mine[:, :half] + other[:, :half].astype(jnp.float32)
    up = mine[:, half:] + other[:, half:].astype(jnp.float32)
    result = (gate / (1.0 + jnp.exp(-gate)) * up).astype(jnp.bfloat16)
    place = lax.broadcasted_iota(jnp.int32, (half, half), 0)
    column = lax.broadcasted_iota(jnp.int32, (half, half), 1)
    group = column // ROWS
    wanted = (group % 2 * PAIRS + group // 2) * ROWS + column % ROWS
    move = (place == wanted).astype(jnp.float32).astype(jnp.bfloat16)
    out[...] = jnp.dot(result, move, preferred_element_type=jnp.float32).astype(jnp.bfloat16)


def finish(core, mine, both):
    vmem = pl.BlockSpec(memory_space=pltpu.VMEM)
    return pl.pallas_call(
        finish_kernel,
        in_specs=[pl.BlockSpec(memory_space=pltpu.SMEM), vmem, vmem],
        out_specs=vmem,
        out_shape=jax.ShapeDtypeStruct((TOKENS // GROUPS, GROUPS * ROWS), jnp.bfloat16),
        compiler_params=pltpu.CompilerParams(vmem_limit_bytes=32 * 2**20),
        cost_estimate=pl.CostEstimate(flops=2**20, bytes_accessed=3 * 2**19, transcendentals=2**16),
        name="finish",
    )(core, mine, both)


def exchange_weights(blocks, other, tokens):
    weights = jnp.concatenate([part[:HELD].reshape(PAIRS, 2 * ROWS, 2 * WIDTH) for part in (other, blocks)], axis=1)
    weights = lax.all_to_all(weights, "y", 0, 0, tiled=True)
    return *project_own(weights, tokens), jnp.zeros((GROUPS, SIDE, LANES), jnp.bfloat16)


def exchange_shrunk(blocks, other, tokens):
    side, total, weights = shrink(blocks, other, tokens)
    return total, weights, lax.all_to_all(side, TENSOR, 0, 0, tiled=True)


def base_term(total, weights, side, near_tokens):
    parts = project_near(total, weights, near_tokens)
    parts = lax.all_to_all(parts.reshape(GROUPS, TOKENS // GROUPS, -1), TENSOR, 0, 0, tiled=True)
    return tuple(add_up(parts))


def adapter_term(total, weights, side, near_tokens):
    copies = copies_of(side, lax.axis_size("xl") * lax.axis_size("z"))
    shrunk = lax.all_to_all(copies, ("z", "xl"), 0, 0, tiled=True)
    return tuple(grow(spread_out(side), shrunk))


def per_device(tokens, gate_ids, up_ids, gate_powers, up_powers, gate_b, up_b, gate_a, up_a):
    core = lax.axis_index("c").astype(jnp.int32)
    pairs = [(xl * 4 + 2 + xh, (1 - xl) * 4 + 2 + 1 - xh) for xl in range(2) for xh in range(2)]
    near_tokens = lax.ppermute(tokens, ("xl", "c", "xh"), pairs)
    own = lax.axis_index("xh").astype(jnp.int32).reshape(1)
    blocks = decode(own, gate_ids, up_ids, gate_powers, up_powers, gate_b, up_b, gate_a, up_a)
    other = lax.ppermute(blocks, "c", [(0, 1), (1, 0)])
    total, weights, side = lax.cond(core == 0, exchange_shrunk, exchange_weights, blocks, other, tokens)
    mine, theirs = lax.cond(core == 0, adapter_term, base_term, total, weights, side, near_tokens)
    return finish(core.reshape(1), mine, lax.all_gather(theirs, "c", axis=0))


def solution(mesh):
    split = Mesh(mesh.devices.reshape(2, 16, 2, 4, 2), ("xl", "z", "c", "y", "xh"))
    rows = P(FSDP + TENSOR, None)
    placed = (P(None, TENSOR), rows, rows, rows, rows, rows, rows, P(FSDP, TENSOR), P(FSDP, TENSOR))
    return jax.shard_map(per_device, mesh=split, in_specs=placed, out_specs=P(TENSOR, FSDP), check_vma=False)
```

```python
import jax
import jax.numpy as jnp
import ml_dtypes
from jax import lax
from jax.experimental import pallas as pl
from jax.experimental.pallas import tpu as pltpu
from jax.sharding import Mesh
from jax.sharding import PartitionSpec as P

BLOCK = 64
RANK = 128
GROUPS = 8
ROWS = 32
WIDTH = 1024
TOKENS = 1344
LANES = 128
PAIRS = 4
PIECES = 2
HELD = 2 * 4 * 32
SIDE = 144

NF4_LEVELS = (
    -1.0,
    -0.6961928009986877,
    -0.5250730514526367,
    -0.39491748809814453,
    -0.28444138169288635,
    -0.18477343022823334,
    -0.09105003625154495,
    0.0,
    0.07958029955625534,
    0.16093020141124725,
    0.24611230194568634,
    0.3379152408981323,
    0.44070982933044434,
    0.5626170039176941,
    0.7229568362236023,
    1.0,
)
LEVELS = tuple(float(ml_dtypes.bfloat16(v)) for v in NF4_LEVELS)

FSDP = ("xl", "z", "c")
TENSOR = ("y", "xh")
def pick(ids, low, high):
    if high - low == 1:
        return jnp.full(ids.shape, LEVELS[low], jnp.bfloat16)
    middle = (low + high) // 2
    return jnp.where(ids < jnp.int16(middle), pick(ids, low, middle), pick(ids, middle, high))


def lookup(table, index):
    return jnp.take_along_axis(table, index, axis=1, mode="promise_in_bounds")


def decode_kernel(own, gate_ids, up_ids, gate_powers, up_powers, gate_b, up_b, gate_a, up_a, out, ids, small, thin, ready, near, sent):
    extra, stores = [], []
    for p, (powers, factor, a) in enumerate(((gate_powers, gate_b, gate_a), (up_powers, up_b, up_a))):
        extra.append(pltpu.make_async_copy(powers, small.at[p], near.at[p]))
        extra.append(pltpu.make_async_copy(a, thin.at[p], near.at[2 + p]))
        for h in range(2):
            place = out.at[pl.ds(HELD, 16), pl.ds((2 * p + h) * RANK, RANK)]
            stores.append(pltpu.make_async_copy(factor.at[pl.ds(h * 16, 16)], place, sent.at[2 * p + h]))
    loads, groups = [], []
    for k in range(GROUPS):
        group = k // 2 * 2 + (own[0] + k % 2) % 2
        groups.append(group)
        columns = pl.ds(pl.multiple_of(group * WIDTH, WIDTH), WIDTH)
        loads.append(
            [pltpu.make_async_copy(ref.at[:, columns], ids.at[p, k], ready.at[p, k]) for p, ref in enumerate((gate_ids, up_ids))]
        )
    for copy in extra + sum(loads, []) + stores:
        copy.start()
    for copy in extra:
        copy.wait()
    rows = jnp.concatenate([thin[0].astype(jnp.float32), thin[1].astype(jnp.float32), jnp.zeros((12, WIDTH), jnp.float32)], axis=0)
    out[pl.ds(HELD, 16), pl.ds(WIDTH, WIDTH)] = rows.astype(jnp.bfloat16)
    half = lax.broadcasted_iota(jnp.int32, (ROWS, LANES), 1) // BLOCK
    scales = [(jnp.int32(1) << (small[p] + 8)).astype(jnp.float32) * 2.0**-8 for p in range(2)]
    for k in range(GROUPS):
        for p in range(2):
            loads[k][p].wait()
            rows = pl.ds(k // 2 * 2 * ROWS + p * ROWS, ROWS)
            for chunk in range(WIDTH // LANES):
                level = pick(ids[p, k, :, pl.ds(chunk * LANES, LANES)].astype(jnp.int16), 0, len(LEVELS))
                scale = lookup(scales[p], half + (groups[k] * (WIDTH // BLOCK) + chunk * (LANES // BLOCK)))
                columns = pl.ds(k % 2 * WIDTH + chunk * LANES, LANES)
                out[rows, columns] = level * scale.astype(jnp.bfloat16)
    for store in stores:
        store.wait()


def decode(*args):
    shape = (HELD + 16, 2 * WIDTH)
    hbm = pl.BlockSpec(memory_space=pltpu.HBM)
    return pl.pallas_call(
        decode_kernel,
        in_specs=[pl.BlockSpec(memory_space=pltpu.SMEM)] + [hbm] * 8,
        out_specs=pl.BlockSpec(memory_space=pltpu.VMEM),
        out_shape=jax.ShapeDtypeStruct(shape, jnp.bfloat16),
        scratch_shapes=[
            pltpu.VMEM((2, GROUPS, ROWS, WIDTH), jnp.int32),
            pltpu.VMEM((2, ROWS, LANES), jnp.int32),
            pltpu.VMEM((2, 2, WIDTH), jnp.bfloat16),
            pltpu.SemaphoreType.DMA((2, GROUPS)),
            pltpu.SemaphoreType.DMA((4,)),
            pltpu.SemaphoreType.DMA((4,)),
        ],
        compiler_params=pltpu.CompilerParams(vmem_limit_bytes=62 * 2**20),
        cost_estimate=pl.CostEstimate(flops=2**24, bytes_accessed=3 * 2**20, transcendentals=0),
        name="decode",
    )(*args)


DIMS = (((1,), (1,)), ((), ()))


def project_own_kernel(weights, tokens, out, rest, merged):
    part = PAIRS * ROWS
    for q in range(4):
        merged[pl.ds(q * part, part), :] = weights[:, pl.ds(q * ROWS, ROWS), pl.ds(0, WIDTH)].reshape(part, WIDTH)
        rest[pl.ds(q * part, part), :] = weights[:, pl.ds(q * ROWS, ROWS), pl.ds(WIDTH, WIDTH)].reshape(part, WIDTH)
    out[...] = lax.dot_general(tokens[...], merged[...], DIMS, preferred_element_type=jnp.float32)


def project_own(weights, tokens):
    place = pl.BlockSpec(memory_space=pltpu.VMEM)
    columns = 4 * PAIRS * ROWS
    return pl.pallas_call(
        project_own_kernel,
        in_specs=[place, place],
        out_specs=[place, place],
        out_shape=[
            jax.ShapeDtypeStruct((TOKENS, columns), jnp.float32),
            jax.ShapeDtypeStruct((columns, WIDTH), jnp.bfloat16),
        ],
        scratch_shapes=[pltpu.VMEM((columns, WIDTH), jnp.bfloat16)],
        compiler_params=pltpu.CompilerParams(vmem_limit_bytes=32 * 2**20),
        cost_estimate=pl.CostEstimate(flops=TOKENS * 1024 * 1024, bytes_accessed=8 * 2**20, transcendentals=0),
        name="project_own",
    )(weights, tokens)


def project_near_kernel(total, weights, tokens, out, held, ready):
    part = TOKENS // PIECES
    loads = []
    for i in range(PIECES):
        rows = pl.ds(i * part, part)
        loads.append(pltpu.make_async_copy(tokens.at[rows], held.at[rows], ready.at[i]))
        loads[-1].start()
    for i in range(PIECES):
        rows = pl.ds(i * part, part)
        loads[i].wait()
        product = lax.dot_general(held[rows, :], weights[...], DIMS, preferred_element_type=jnp.float32)
        out[rows, :] = (total[rows, :] + product).astype(jnp.bfloat16)


def project_near(total, weights, tokens):
    place = pl.BlockSpec(memory_space=pltpu.VMEM)
    return pl.pallas_call(
        project_near_kernel,
        in_specs=[place, place, pl.BlockSpec(memory_space=pltpu.HBM)],
        out_specs=place,
        out_shape=jax.ShapeDtypeStruct(total.shape, jnp.bfloat16),
        scratch_shapes=[pltpu.VMEM((TOKENS, WIDTH), jnp.bfloat16), pltpu.SemaphoreType.DMA((PIECES,))],
        compiler_params=pltpu.CompilerParams(vmem_limit_bytes=32 * 2**20),
        cost_estimate=pl.CostEstimate(flops=TOKENS * 1024 * 1024, bytes_accessed=8 * 2**20, transcendentals=0),
        name="project_near",
    )(total, weights, tokens)


def add_up_kernel(parts, mine, theirs):
    part = PAIRS * ROWS
    for x in range(2):
        total = parts[x].astype(jnp.float32)
        for y in range(1, PAIRS):
            total = total + parts[2 * y + x].astype(jnp.float32)
        for q in range(4):
            to = theirs if q < 2 else mine
            to[:, pl.ds((q % 2 * 2 + x) * part, part)] = total[:, q * part : (q + 1) * part].astype(to.dtype)


def add_up(parts):
    shape = (parts.shape[1], parts.shape[2])
    return pl.pallas_call(
        add_up_kernel,
        out_shape=[jax.ShapeDtypeStruct(shape, jnp.float32), jax.ShapeDtypeStruct(shape, jnp.bfloat16)],
        compiler_params=pltpu.CompilerParams(vmem_limit_bytes=32 * 2**20),
        cost_estimate=pl.CostEstimate(flops=2**21, bytes_accessed=3 * 2**20, transcendentals=0),
        name="add_up",
    )(parts)


def shrink_kernel(first, second, tokens, out, *rest):
    a = [block[:, pl.ds(WIDTH, WIDTH)].astype(jnp.float32)[0:4] for block in (first, second)]
    a = jnp.concatenate(a, axis=0).astype(jnp.bfloat16)
    count = TOKENS // GROUPS
    step = pl.program_id(0) * tokens.shape[0]
    for k in range(tokens.shape[0]):
        for c, block in enumerate((first, second)):
            for h in range(4):
                out[step + k, pl.ds(c * 2 * ROWS + h * 16, 16), :] = block[:, pl.ds(h * RANK, RANK)]
        product = lax.dot_general(a, tokens[k], (((1,), (1,)), ((), ())), preferred_element_type=jnp.float32)
        high = jnp.concatenate([product[:, LANES:], jnp.zeros((8, 2 * LANES - count), jnp.float32)], axis=1)
        both = jnp.concatenate([product[:, :LANES], high], axis=0)
        out[step + k, pl.ds(4 * ROWS, 16), :] = both.astype(jnp.bfloat16)


def shrink(first, second, tokens, steps=2):
    side = pl.BlockSpec((16, 2 * WIDTH), lambda i: (HELD // 16, 0))
    columns = 4 * PAIRS * ROWS
    room = pl.BlockSpec(memory_space=pl.ANY)
    return pl.pallas_call(
        shrink_kernel,
        grid=(steps,),
        in_specs=[side, side, pl.BlockSpec((GROUPS // steps, TOKENS // GROUPS, WIDTH), lambda i: (i, 0, 0))],
        out_specs=[pl.BlockSpec((GROUPS, SIDE, LANES), lambda i: (0, 0, 0)), room, room],
        out_shape=[
            jax.ShapeDtypeStruct((GROUPS, SIDE, LANES), jnp.bfloat16),
            jax.ShapeDtypeStruct((TOKENS, columns), jnp.float32),
            jax.ShapeDtypeStruct((columns, WIDTH), jnp.bfloat16),
        ],
        compiler_params=pltpu.CompilerParams(vmem_limit_bytes=40 * 2**20),
        cost_estimate=pl.CostEstimate(flops=2**24, bytes_accessed=3 * 2**20, transcendentals=0),
        name="shrink",
    )(first, second, tokens.reshape(GROUPS, TOKENS // GROUPS, WIDTH))


def copies_kernel(side, out):
    total = side[0, pl.ds(4 * ROWS, 16), :].astype(jnp.float32)
    for k in range(1, GROUPS):
        total = total + side[k, pl.ds(4 * ROWS, 16), :].astype(jnp.float32)
    for place in range(out.shape[0]):
        out[place] = total.astype(jnp.bfloat16)


def copies_of(side, count):
    return pl.pallas_call(
        copies_kernel,
        out_shape=jax.ShapeDtypeStruct((count, 16, LANES), jnp.bfloat16),
        cost_estimate=pl.CostEstimate(flops=2**14, bytes_accessed=2**19, transcendentals=0),
        name="copies",
    )(side)


def spread_kernel(side, out):
    rank = lax.broadcasted_iota(jnp.int32, (RANK, 2 * RANK), 0)
    place = lax.broadcasted_iota(jnp.int32, (RANK, 2 * RANK), 1)
    slot = place // 4
    owner = slot // 2 % 2 * 32 + slot // 4 * 2 + slot % 2
    for q in range(4):
        hit = (place % 4 // 2 == q % 2) & (owner * 2 + place % 2 == rank)
        factor = jnp.concatenate([side[k, pl.ds(q * ROWS, ROWS), :] for k in (0, 2, 4, 6, 1, 3, 5, 7)], axis=0)
        out[q] = jnp.dot(
            factor, hit.astype(jnp.float32).astype(jnp.bfloat16), preferred_element_type=jnp.float32
        ).astype(jnp.bfloat16)


def spread_out(side):
    return pl.pallas_call(
        spread_kernel,
        out_shape=jax.ShapeDtypeStruct((4, GROUPS * ROWS, 2 * RANK), jnp.bfloat16),
        compiler_params=pltpu.CompilerParams(vmem_limit_bytes=16 * 2**20),
        cost_estimate=pl.CostEstimate(flops=2**26, bytes_accessed=2**20, transcendentals=0),
        name="spread_out",
    )(side)


def grow_kernel(factors, shrunk, mine, theirs):
    count = TOKENS // GROUPS
    values = shrunk[...].astype(jnp.float32)
    low = values[:, 0:8, :].reshape(2 * RANK, LANES).T.astype(jnp.bfloat16)
    high = values[:, 8:16, :].reshape(2 * RANK, LANES).T.astype(jnp.bfloat16)
    half = GROUPS * ROWS
    for q in range(4):
        to = mine if q < 2 else theirs
        columns = pl.ds(q % 2 * half, half)
        to[pl.ds(0, LANES), columns] = lax.dot_general(
            low, factors[q], (((1,), (1,)), ((), ())), preferred_element_type=jnp.float32
        ).astype(to.dtype)
        to[pl.ds(LANES, count - LANES), columns] = lax.dot_general(
            high, factors[q], (((1,), (1,)), ((), ())), preferred_element_type=jnp.float32
        )[: count - LANES].astype(to.dtype)


def grow(factors, shrunk):
    shape = (TOKENS // GROUPS, 2 * GROUPS * ROWS)
    return pl.pallas_call(
        grow_kernel,
        out_shape=[jax.ShapeDtypeStruct(shape, jnp.float32), jax.ShapeDtypeStruct(shape, jnp.bfloat16)],
        compiler_params=pltpu.CompilerParams(vmem_limit_bytes=32 * 2**20),
        cost_estimate=pl.CostEstimate(flops=2**25, bytes_accessed=2**20, transcendentals=0),
        name="grow",
    )(factors, shrunk)


def finish_kernel(core, mine, both, out):
    half = GROUPS * ROWS
    other = both.at[1 - core[0]]
    gate = mine[:, :half] + other[:, :half].astype(jnp.float32)
    up = mine[:, half:] + other[:, half:].astype(jnp.float32)
    result = (gate / (1.0 + jnp.exp(-gate)) * up).astype(jnp.bfloat16)
    place = lax.broadcasted_iota(jnp.int32, (half, half), 0)
    column = lax.broadcasted_iota(jnp.int32, (half, half), 1)
    group = column // ROWS
    wanted = (group % 2 * PAIRS + group // 2) * ROWS + column % ROWS
    move = (place == wanted).astype(jnp.float32).astype(jnp.bfloat16)
    out[...] = jnp.dot(result, move, preferred_element_type=jnp.float32).astype(jnp.bfloat16)


def finish(core, mine, both):
    vmem = pl.BlockSpec(memory_space=pltpu.VMEM)
    return pl.pallas_call(
        finish_kernel,
        in_specs=[pl.BlockSpec(memory_space=pltpu.SMEM), vmem, vmem],
        out_specs=vmem,
        out_shape=jax.ShapeDtypeStruct((TOKENS // GROUPS, GROUPS * ROWS), jnp.bfloat16),
        compiler_params=pltpu.CompilerParams(vmem_limit_bytes=32 * 2**20),
        cost_estimate=pl.CostEstimate(flops=2**20, bytes_accessed=3 * 2**19, transcendentals=2**16),
        name="finish",
    )(core, mine, both)


def exchange_weights(blocks, other, tokens):
    weights = jnp.concatenate([part[:HELD].reshape(PAIRS, 2 * ROWS, 2 * WIDTH) for part in (other, blocks)], axis=1)
    weights = lax.all_to_all(weights, "y", 0, 0, tiled=True)
    return *project_own(weights, tokens), jnp.zeros((GROUPS, SIDE, LANES), jnp.bfloat16)


def exchange_shrunk(blocks, other, tokens):
    side, total, weights = shrink(blocks, other, tokens)
    return total, weights, lax.all_to_all(side, TENSOR, 0, 0, tiled=True)


def base_term(total, weights, side, near_tokens):
    parts = project_near(total, weights, near_tokens)
    parts = lax.all_to_all(parts.reshape(GROUPS, TOKENS // GROUPS, -1), TENSOR, 0, 0, tiled=True)
    return tuple(add_up(parts))


def adapter_term(total, weights, side, near_tokens):
    copies = copies_of(side, lax.axis_size("xl") * lax.axis_size("z"))
    shrunk = lax.all_to_all(copies, ("z", "xl"), 0, 0, tiled=True)
    return tuple(grow(spread_out(side), shrunk))


def per_device(tokens, gate_ids, up_ids, gate_powers, up_powers, gate_b, up_b, gate_a, up_a):
    core = lax.axis_index("c").astype(jnp.int32)
    pairs = [(xl * 4 + 2 + xh, (1 - xl) * 4 + 2 + 1 - xh) for xl in range(2) for xh in range(2)]
    near_tokens = lax.ppermute(tokens, ("xl", "c", "xh"), pairs)
    own = lax.axis_index("xh").astype(jnp.int32).reshape(1)
    blocks = decode(own, gate_ids, up_ids, gate_powers, up_powers, gate_b, up_b, gate_a, up_a)
    other = lax.ppermute(blocks, "c", [(0, 1), (1, 0)])
    total, weights, side = lax.cond(core == 0, exchange_shrunk, exchange_weights, blocks, other, tokens)
    mine, theirs = lax.cond(core == 0, adapter_term, base_term, total, weights, side, near_tokens)
    return finish(core.reshape(1), mine, lax.all_gather(theirs, "c", axis=0))


def solution(mesh):
    split = Mesh(mesh.devices.reshape(2, 16, 2, 4, 2), ("xl", "z", "c", "y", "xh"))
    rows = P(FSDP + TENSOR, None)
    placed = (P(None, TENSOR), rows, rows, rows, rows, rows, rows, P(FSDP, TENSOR), P(FSDP, TENSOR))
    return jax.shard_map(per_device, mesh=split, in_specs=placed, out_specs=P(TENSOR, FSDP), check_vma=False)
```

```python
import jax
import jax.numpy as jnp
import ml_dtypes
from jax import lax
from jax.experimental import pallas as pl
from jax.experimental.pallas import tpu as pltpu
from jax.sharding import Mesh
from jax.sharding import PartitionSpec as P

BLOCK = 64
RANK = 128
GROUPS = 8
ROWS = 32
WIDTH = 1024
TOKENS = 1344
LANES = 128
PAIRS = 4
PIECES = 2
HELD = 2 * 4 * 32
SIDE = 144

NF4_LEVELS = (
    -1.0,
    -0.6961928009986877,
    -0.5250730514526367,
    -0.39491748809814453,
    -0.28444138169288635,
    -0.18477343022823334,
    -0.09105003625154495,
    0.0,
    0.07958029955625534,
    0.16093020141124725,
    0.24611230194568634,
    0.3379152408981323,
    0.44070982933044434,
    0.5626170039176941,
    0.7229568362236023,
    1.0,
)
LEVELS = tuple(float(ml_dtypes.bfloat16(v)) for v in NF4_LEVELS)

FSDP = ("xl", "z", "c")
TENSOR = ("y", "xh")
def pick(ids, low, high):
    if high - low == 1:
        return jnp.full(ids.shape, LEVELS[low], jnp.bfloat16)
    middle = (low + high) // 2
    return jnp.where(ids < jnp.int16(middle), pick(ids, low, middle), pick(ids, middle, high))


def lookup(table, index):
    return jnp.take_along_axis(table, index, axis=1, mode="promise_in_bounds")


def decode_kernel(own, gate_ids, up_ids, gate_powers, up_powers, gate_b, up_b, gate_a, up_a, out, ids, small, thin, ready, near, sent):
    extra, stores = [], []
    for p, (powers, factor, a) in enumerate(((gate_powers, gate_b, gate_a), (up_powers, up_b, up_a))):
        extra.append(pltpu.make_async_copy(powers, small.at[p], near.at[p]))
        extra.append(pltpu.make_async_copy(a, thin.at[p], near.at[2 + p]))
        for h in range(2):
            place = out.at[pl.ds(HELD, 16), pl.ds((2 * p + h) * RANK, RANK)]
            stores.append(pltpu.make_async_copy(factor.at[pl.ds(h * 16, 16)], place, sent.at[2 * p + h]))
    loads, groups = [], []
    for k in range(GROUPS):
        group = k // 2 * 2 + (own[0] + k % 2) % 2
        groups.append(group)
        columns = pl.ds(pl.multiple_of(group * WIDTH, WIDTH), WIDTH)
        loads.append(
            [pltpu.make_async_copy(ref.at[:, columns], ids.at[p, k], ready.at[p, k]) for p, ref in enumerate((gate_ids, up_ids))]
        )
    for copy in extra + sum(loads, []) + stores:
        copy.start()
    for copy in extra:
        copy.wait()
    rows = jnp.concatenate([thin[0].astype(jnp.float32), thin[1].astype(jnp.float32), jnp.zeros((12, WIDTH), jnp.float32)], axis=0)
    out[pl.ds(HELD, 16), pl.ds(WIDTH, WIDTH)] = rows.astype(jnp.bfloat16)
    half = lax.broadcasted_iota(jnp.int32, (ROWS, LANES), 1) // BLOCK
    scales = [(jnp.int32(1) << (small[p] + 8)).astype(jnp.float32) * 2.0**-8 for p in range(2)]
    for k in range(GROUPS):
        for p in range(2):
            loads[k][p].wait()
            rows = pl.ds(k // 2 * 2 * ROWS + p * ROWS, ROWS)
            for chunk in range(WIDTH // LANES):
                level = pick(ids[p, k, :, pl.ds(chunk * LANES, LANES)].astype(jnp.int16), 0, len(LEVELS))
                scale = lookup(scales[p], half + (groups[k] * (WIDTH // BLOCK) + chunk * (LANES // BLOCK)))
                columns = pl.ds(k % 2 * WIDTH + chunk * LANES, LANES)
                out[rows, columns] = level * scale.astype(jnp.bfloat16)
    for store in stores:
        store.wait()


def decode(*args):
    shape = (HELD + 16, 2 * WIDTH)
    hbm = pl.BlockSpec(memory_space=pltpu.HBM)
    return pl.pallas_call(
        decode_kernel,
        in_specs=[pl.BlockSpec(memory_space=pltpu.SMEM)] + [hbm] * 8,
        out_specs=pl.BlockSpec(memory_space=pltpu.VMEM),
        out_shape=jax.ShapeDtypeStruct(shape, jnp.bfloat16),
        scratch_shapes=[
            pltpu.VMEM((2, GROUPS, ROWS, WIDTH), jnp.int32),
            pltpu.VMEM((2, ROWS, LANES), jnp.int32),
            pltpu.VMEM((2, 2, WIDTH), jnp.bfloat16),
            pltpu.SemaphoreType.DMA((2, GROUPS)),
            pltpu.SemaphoreType.DMA((4,)),
            pltpu.SemaphoreType.DMA((4,)),
        ],
        compiler_params=pltpu.CompilerParams(vmem_limit_bytes=62 * 2**20),
        cost_estimate=pl.CostEstimate(flops=2**24, bytes_accessed=3 * 2**20, transcendentals=0),
        name="decode",
    )(*args)


DIMS = (((1,), (1,)), ((), ()))


def project_own_kernel(weights, tokens, out, rest, merged):
    part = PAIRS * ROWS
    for q in range(4):
        merged[pl.ds(q * part, part), :] = weights[:, pl.ds(q * ROWS, ROWS), pl.ds(0, WIDTH)].reshape(part, WIDTH)
        rest[pl.ds(q * part, part), :] = weights[:, pl.ds(q * ROWS, ROWS), pl.ds(WIDTH, WIDTH)].reshape(part, WIDTH)
    out[...] = lax.dot_general(tokens[...], merged[...], DIMS, preferred_element_type=jnp.float32)


def project_own(weights, tokens):
    place = pl.BlockSpec(memory_space=pltpu.VMEM)
    columns = 4 * PAIRS * ROWS
    return pl.pallas_call(
        project_own_kernel,
        in_specs=[place, place],
        out_specs=[place, place],
        out_shape=[
            jax.ShapeDtypeStruct((TOKENS, columns), jnp.float32),
            jax.ShapeDtypeStruct((columns, WIDTH), jnp.bfloat16),
        ],
        scratch_shapes=[pltpu.VMEM((columns, WIDTH), jnp.bfloat16)],
        compiler_params=pltpu.CompilerParams(vmem_limit_bytes=32 * 2**20),
        cost_estimate=pl.CostEstimate(flops=TOKENS * 1024 * 1024, bytes_accessed=8 * 2**20, transcendentals=0),
        name="project_own",
    )(weights, tokens)


def project_near_kernel(total, weights, tokens, out, held, ready):
    part = TOKENS // PIECES
    loads = []
    for i in range(PIECES):
        rows = pl.ds(i * part, part)
        loads.append(pltpu.make_async_copy(tokens.at[rows], held.at[rows], ready.at[i]))
        loads[-1].start()
    for i in range(PIECES):
        rows = pl.ds(i * part, part)
        loads[i].wait()
        product = lax.dot_general(held[rows, :], weights[...], DIMS, preferred_element_type=jnp.float32)
        out[rows, :] = (total[rows, :] + product).astype(jnp.bfloat16)


def project_near(total, weights, tokens):
    place = pl.BlockSpec(memory_space=pltpu.VMEM)
    return pl.pallas_call(
        project_near_kernel,
        in_specs=[place, place, pl.BlockSpec(memory_space=pltpu.HBM)],
        out_specs=place,
        out_shape=jax.ShapeDtypeStruct(total.shape, jnp.bfloat16),
        scratch_shapes=[pltpu.VMEM((TOKENS, WIDTH), jnp.bfloat16), pltpu.SemaphoreType.DMA((PIECES,))],
        compiler_params=pltpu.CompilerParams(vmem_limit_bytes=32 * 2**20),
        cost_estimate=pl.CostEstimate(flops=TOKENS * 1024 * 1024, bytes_accessed=8 * 2**20, transcendentals=0),
        name="project_near",
    )(total, weights, tokens)


def add_up_kernel(parts, mine, theirs):
    part = PAIRS * ROWS
    totals = []
    for x in range(2):
        total = parts[x].astype(jnp.float32)
        for y in range(1, PAIRS):
            total = total + parts[2 * y + x].astype(jnp.float32)
        totals.append(total)
    for q in range(4):
        to = theirs if q < 2 else mine
        pieces = [totals[x][:, q * part + y * ROWS : q * part + (y + 1) * ROWS] for y in range(PAIRS) for x in range(2)]
        to[:, pl.ds(q % 2 * 2 * part, 2 * part)] = jnp.concatenate(pieces, axis=1).astype(to.dtype)


def add_up(parts):
    shape = (parts.shape[1], parts.shape[2])
    return pl.pallas_call(
        add_up_kernel,
        out_shape=[jax.ShapeDtypeStruct(shape, jnp.float32), jax.ShapeDtypeStruct(shape, jnp.bfloat16)],
        compiler_params=pltpu.CompilerParams(vmem_limit_bytes=32 * 2**20),
        cost_estimate=pl.CostEstimate(flops=2**21, bytes_accessed=3 * 2**20, transcendentals=0),
        name="add_up",
    )(parts)


def shrink_kernel(first, second, tokens, out, *rest):
    a = [block[:, pl.ds(WIDTH, WIDTH)].astype(jnp.float32)[0:4] for block in (first, second)]
    a = jnp.concatenate(a, axis=0).astype(jnp.bfloat16)
    count = TOKENS // GROUPS
    step = pl.program_id(0) * tokens.shape[0]
    for k in range(tokens.shape[0]):
        for c, block in enumerate((first, second)):
            for h in range(4):
                out[step + k, pl.ds(c * 2 * ROWS + h * 16, 16), :] = block[:, pl.ds(h * RANK, RANK)]
        product = lax.dot_general(a, tokens[k], (((1,), (1,)), ((), ())), preferred_element_type=jnp.float32)
        high = jnp.concatenate([product[:, LANES:], jnp.zeros((8, 2 * LANES - count), jnp.float32)], axis=1)
        both = jnp.concatenate([product[:, :LANES], high], axis=0)
        out[step + k, pl.ds(4 * ROWS, 16), :] = both.astype(jnp.bfloat16)


def shrink(first, second, tokens, steps=2):
    side = pl.BlockSpec((16, 2 * WIDTH), lambda i: (HELD // 16, 0))
    columns = 4 * PAIRS * ROWS
    room = pl.BlockSpec(memory_space=pl.ANY)
    return pl.pallas_call(
        shrink_kernel,
        grid=(steps,),
        in_specs=[side, side, pl.BlockSpec((GROUPS // steps, TOKENS // GROUPS, WIDTH), lambda i: (i, 0, 0))],
        out_specs=[pl.BlockSpec((GROUPS, SIDE, LANES), lambda i: (0, 0, 0)), room, room],
        out_shape=[
            jax.ShapeDtypeStruct((GROUPS, SIDE, LANES), jnp.bfloat16),
            jax.ShapeDtypeStruct((TOKENS, columns), jnp.float32),
            jax.ShapeDtypeStruct((columns, WIDTH), jnp.bfloat16),
        ],
        compiler_params=pltpu.CompilerParams(vmem_limit_bytes=40 * 2**20),
        cost_estimate=pl.CostEstimate(flops=2**24, bytes_accessed=3 * 2**20, transcendentals=0),
        name="shrink",
    )(first, second, tokens.reshape(GROUPS, TOKENS // GROUPS, WIDTH))


def copies_kernel(side, out):
    total = side[0, pl.ds(4 * ROWS, 16), :].astype(jnp.float32)
    for k in range(1, GROUPS):
        total = total + side[k, pl.ds(4 * ROWS, 16), :].astype(jnp.float32)
    for place in range(out.shape[0]):
        out[place] = total.astype(jnp.bfloat16)


def copies_of(side, count):
    return pl.pallas_call(
        copies_kernel,
        out_shape=jax.ShapeDtypeStruct((count, 16, LANES), jnp.bfloat16),
        cost_estimate=pl.CostEstimate(flops=2**14, bytes_accessed=2**19, transcendentals=0),
        name="copies",
    )(side)


def spread_kernel(side, out):
    rank = lax.broadcasted_iota(jnp.int32, (RANK, 2 * RANK), 0)
    place = lax.broadcasted_iota(jnp.int32, (RANK, 2 * RANK), 1)
    slot = place // 4
    owner = slot // 2 % 2 * 32 + slot // 4 * 2 + slot % 2
    for q in range(4):
        hit = (place % 4 // 2 == q % 2) & (owner * 2 + place % 2 == rank)
        factor = jnp.concatenate([side[k, pl.ds(q * ROWS, ROWS), :] for k in range(GROUPS)], axis=0)
        out[q] = jnp.dot(
            factor, hit.astype(jnp.float32).astype(jnp.bfloat16), preferred_element_type=jnp.float32
        ).astype(jnp.bfloat16)


def spread_out(side):
    return pl.pallas_call(
        spread_kernel,
        out_shape=jax.ShapeDtypeStruct((4, GROUPS * ROWS, 2 * RANK), jnp.bfloat16),
        compiler_params=pltpu.CompilerParams(vmem_limit_bytes=16 * 2**20),
        cost_estimate=pl.CostEstimate(flops=2**26, bytes_accessed=2**20, transcendentals=0),
        name="spread_out",
    )(side)


def grow_kernel(factors, shrunk, mine, theirs):
    count = TOKENS // GROUPS
    values = shrunk[...].astype(jnp.float32)
    low = values[:, 0:8, :].reshape(2 * RANK, LANES).T.astype(jnp.bfloat16)
    high = values[:, 8:16, :].reshape(2 * RANK, LANES).T.astype(jnp.bfloat16)
    half = GROUPS * ROWS
    for q in range(4):
        to = mine if q < 2 else theirs
        columns = pl.ds(q % 2 * half, half)
        to[pl.ds(0, LANES), columns] = lax.dot_general(
            low, factors[q], (((1,), (1,)), ((), ())), preferred_element_type=jnp.float32
        ).astype(to.dtype)
        to[pl.ds(LANES, count - LANES), columns] = lax.dot_general(
            high, factors[q], (((1,), (1,)), ((), ())), preferred_element_type=jnp.float32
        )[: count - LANES].astype(to.dtype)


def grow(factors, shrunk):
    shape = (TOKENS // GROUPS, 2 * GROUPS * ROWS)
    return pl.pallas_call(
        grow_kernel,
        out_shape=[jax.ShapeDtypeStruct(shape, jnp.float32), jax.ShapeDtypeStruct(shape, jnp.bfloat16)],
        compiler_params=pltpu.CompilerParams(vmem_limit_bytes=32 * 2**20),
        cost_estimate=pl.CostEstimate(flops=2**25, bytes_accessed=2**20, transcendentals=0),
        name="grow",
    )(factors, shrunk)


def finish_kernel(core, mine, both, out):
    half = GROUPS * ROWS
    other = both.at[1 - core[0]]
    gate = mine[:, :half] + other[:, :half].astype(jnp.float32)
    up = mine[:, half:] + other[:, half:].astype(jnp.float32)
    out[...] = (gate / (1.0 + jnp.exp(-gate)) * up).astype(jnp.bfloat16)


def finish(core, mine, both):
    vmem = pl.BlockSpec(memory_space=pltpu.VMEM)
    return pl.pallas_call(
        finish_kernel,
        in_specs=[pl.BlockSpec(memory_space=pltpu.SMEM), vmem, vmem],
        out_specs=vmem,
        out_shape=jax.ShapeDtypeStruct((TOKENS // GROUPS, GROUPS * ROWS), jnp.bfloat16),
        compiler_params=pltpu.CompilerParams(vmem_limit_bytes=32 * 2**20),
        cost_estimate=pl.CostEstimate(flops=2**20, bytes_accessed=3 * 2**19, transcendentals=2**16),
        name="finish",
    )(core, mine, both)


def exchange_weights(blocks, other, tokens):
    weights = jnp.concatenate([part[:HELD].reshape(PAIRS, 2 * ROWS, 2 * WIDTH) for part in (other, blocks)], axis=1)
    weights = lax.all_to_all(weights, "y", 0, 0, tiled=True)
    return *project_own(weights, tokens), jnp.zeros((GROUPS, SIDE, LANES), jnp.bfloat16)


def exchange_shrunk(blocks, other, tokens):
    side, total, weights = shrink(blocks, other, tokens)
    return total, weights, lax.all_to_all(side, TENSOR, 0, 0, tiled=True)


def base_term(total, weights, side, near_tokens):
    parts = project_near(total, weights, near_tokens)
    parts = lax.all_to_all(parts.reshape(GROUPS, TOKENS // GROUPS, -1), TENSOR, 0, 0, tiled=True)
    return tuple(add_up(parts))


def adapter_term(total, weights, side, near_tokens):
    copies = copies_of(side, lax.axis_size("xl") * lax.axis_size("z"))
    shrunk = lax.all_to_all(copies, ("z", "xl"), 0, 0, tiled=True)
    return tuple(grow(spread_out(side), shrunk))


def per_device(tokens, gate_ids, up_ids, gate_powers, up_powers, gate_b, up_b, gate_a, up_a):
    core = lax.axis_index("c").astype(jnp.int32)
    pairs = [(xl * 4 + 2 + xh, (1 - xl) * 4 + 2 + 1 - xh) for xl in range(2) for xh in range(2)]
    near_tokens = lax.ppermute(tokens, ("xl", "c", "xh"), pairs)
    own = lax.axis_index("xh").astype(jnp.int32).reshape(1)
    blocks = decode(own, gate_ids, up_ids, gate_powers, up_powers, gate_b, up_b, gate_a, up_a)
    other = lax.ppermute(blocks, "c", [(0, 1), (1, 0)])
    total, weights, side = lax.cond(core == 0, exchange_shrunk, exchange_weights, blocks, other, tokens)
    mine, theirs = lax.cond(core == 0, adapter_term, base_term, total, weights, side, near_tokens)
    return finish(core.reshape(1), mine, lax.all_gather(theirs, "c", axis=0))


def solution(mesh):
    split = Mesh(mesh.devices.reshape(2, 16, 2, 4, 2), ("xl", "z", "c", "y", "xh"))
    rows = P(FSDP + TENSOR, None)
    placed = (P(None, TENSOR), rows, rows, rows, rows, rows, rows, P(FSDP, TENSOR), P(FSDP, TENSOR))
    return jax.shard_map(per_device, mesh=split, in_specs=placed, out_specs=P(TENSOR, FSDP), check_vma=False)
```

```python
import jax
import jax.numpy as jnp
import ml_dtypes
from jax import lax
from jax.experimental import pallas as pl
from jax.experimental.pallas import tpu as pltpu
from jax.sharding import Mesh
from jax.sharding import PartitionSpec as P

BLOCK = 64
RANK = 128
GROUPS = 8
ROWS = 32
WIDTH = 1024
TOKENS = 1344
LANES = 128
PAIRS = 4
PIECES = 2
HELD = 2 * 4 * 32
SIDE = 144

NF4_LEVELS = (
    -1.0,
    -0.6961928009986877,
    -0.5250730514526367,
    -0.39491748809814453,
    -0.28444138169288635,
    -0.18477343022823334,
    -0.09105003625154495,
    0.0,
    0.07958029955625534,
    0.16093020141124725,
    0.24611230194568634,
    0.3379152408981323,
    0.44070982933044434,
    0.5626170039176941,
    0.7229568362236023,
    1.0,
)
LEVELS = tuple(float(ml_dtypes.bfloat16(v)) for v in NF4_LEVELS)

FSDP = ("xl", "z", "c")
TENSOR = ("y", "xh")
def pick(ids, low, high):
    if high - low == 1:
        return jnp.full(ids.shape, LEVELS[low], jnp.bfloat16)
    middle = (low + high) // 2
    return jnp.where(ids < jnp.int16(middle), pick(ids, low, middle), pick(ids, middle, high))


def lookup(table, index):
    return jnp.take_along_axis(table, index, axis=1, mode="promise_in_bounds")


def decode_kernel(own, gate_ids, up_ids, gate_powers, up_powers, gate_b, up_b, gate_a, up_a, out, ids, small, thin, ready, near, sent):
    extra, stores = [], []
    for p, (powers, factor, a) in enumerate(((gate_powers, gate_b, gate_a), (up_powers, up_b, up_a))):
        extra.append(pltpu.make_async_copy(powers, small.at[p], near.at[p]))
        extra.append(pltpu.make_async_copy(a, thin.at[p], near.at[2 + p]))
        for h in range(2):
            place = out.at[pl.ds(HELD, 16), pl.ds((2 * p + h) * RANK, RANK)]
            stores.append(pltpu.make_async_copy(factor.at[pl.ds(h * 16, 16)], place, sent.at[2 * p + h]))
    loads, groups = [], []
    for k in range(GROUPS):
        group = k // 2 * 2 + (own[0] + k % 2) % 2
        groups.append(group)
        columns = pl.ds(pl.multiple_of(group * WIDTH, WIDTH), WIDTH)
        loads.append(
            [pltpu.make_async_copy(ref.at[:, columns], ids.at[p, k], ready.at[p, k]) for p, ref in enumerate((gate_ids, up_ids))]
        )
    for copy in extra + sum(loads, []) + stores:
        copy.start()
    for copy in extra:
        copy.wait()
    rows = jnp.concatenate([thin[0].astype(jnp.float32), thin[1].astype(jnp.float32), jnp.zeros((12, WIDTH), jnp.float32)], axis=0)
    out[pl.ds(HELD, 16), pl.ds(WIDTH, WIDTH)] = rows.astype(jnp.bfloat16)
    half = lax.broadcasted_iota(jnp.int32, (ROWS, LANES), 1) // BLOCK
    scales = [(jnp.int32(1) << (small[p] + 8)).astype(jnp.float32) * 2.0**-8 for p in range(2)]
    for k in range(GROUPS):
        for p in range(2):
            loads[k][p].wait()
            rows = pl.ds(k // 2 * 2 * ROWS + p * ROWS, ROWS)
            for chunk in range(WIDTH // LANES):
                level = pick(ids[p, k, :, pl.ds(chunk * LANES, LANES)].astype(jnp.int16), 0, len(LEVELS))
                scale = lookup(scales[p], half + (groups[k] * (WIDTH // BLOCK) + chunk * (LANES // BLOCK)))
                columns = pl.ds(k % 2 * WIDTH + chunk * LANES, LANES)
                out[rows, columns] = level * scale.astype(jnp.bfloat16)
    for store in stores:
        store.wait()


def decode(*args):
    shape = (HELD + 16, 2 * WIDTH)
    hbm = pl.BlockSpec(memory_space=pltpu.HBM)
    return pl.pallas_call(
        decode_kernel,
        in_specs=[pl.BlockSpec(memory_space=pltpu.SMEM)] + [hbm] * 8,
        out_specs=pl.BlockSpec(memory_space=pltpu.VMEM),
        out_shape=jax.ShapeDtypeStruct(shape, jnp.bfloat16),
        scratch_shapes=[
            pltpu.VMEM((2, GROUPS, ROWS, WIDTH), jnp.int32),
            pltpu.VMEM((2, ROWS, LANES), jnp.int32),
            pltpu.VMEM((2, 2, WIDTH), jnp.bfloat16),
            pltpu.SemaphoreType.DMA((2, GROUPS)),
            pltpu.SemaphoreType.DMA((4,)),
            pltpu.SemaphoreType.DMA((4,)),
        ],
        compiler_params=pltpu.CompilerParams(vmem_limit_bytes=62 * 2**20),
        cost_estimate=pl.CostEstimate(flops=2**24, bytes_accessed=3 * 2**20, transcendentals=0),
        name="decode",
    )(*args)


DIMS = (((1,), (1,)), ((), ()))


def project_own_kernel(weights, tokens, out, rest, room, merged):
    part = PAIRS * ROWS
    for q in range(4):
        merged[pl.ds(q * part, part), :] = weights[:, pl.ds(q * ROWS, ROWS), pl.ds(0, WIDTH)].reshape(part, WIDTH)
        rest[pl.ds(q * part, part), :] = weights[:, pl.ds(q * ROWS, ROWS), pl.ds(WIDTH, WIDTH)].reshape(part, WIDTH)
    out[...] = lax.dot_general(tokens[...], merged[...], DIMS, preferred_element_type=jnp.float32)


def project_own(weights, tokens):
    place = pl.BlockSpec(memory_space=pltpu.VMEM)
    columns = 4 * PAIRS * ROWS
    return pl.pallas_call(
        project_own_kernel,
        in_specs=[place, place],
        out_specs=[place, place, pl.BlockSpec(memory_space=pl.ANY)],
        out_shape=[
            jax.ShapeDtypeStruct((TOKENS, columns), jnp.float32),
            jax.ShapeDtypeStruct((columns, WIDTH), jnp.bfloat16),
            jax.ShapeDtypeStruct((GROUPS, SIDE, LANES), jnp.bfloat16),
        ],
        scratch_shapes=[pltpu.VMEM((columns, WIDTH), jnp.bfloat16)],
        compiler_params=pltpu.CompilerParams(vmem_limit_bytes=32 * 2**20),
        cost_estimate=pl.CostEstimate(flops=TOKENS * 1024 * 1024, bytes_accessed=8 * 2**20, transcendentals=0),
        name="project_own",
    )(weights, tokens)


def project_near_kernel(total, weights, tokens, out, held, ready):
    part = TOKENS // PIECES
    loads = []
    for i in range(PIECES):
        rows = pl.ds(i * part, part)
        loads.append(pltpu.make_async_copy(tokens.at[rows], held.at[rows], ready.at[i]))
        loads[-1].start()
    for i in range(PIECES):
        rows = pl.ds(i * part, part)
        loads[i].wait()
        product = lax.dot_general(held[rows, :], weights[...], DIMS, preferred_element_type=jnp.float32)
        out[rows, :] = (total[rows, :] + product).astype(jnp.bfloat16)


def project_near(total, weights, tokens):
    place = pl.BlockSpec(memory_space=pltpu.VMEM)
    return pl.pallas_call(
        project_near_kernel,
        in_specs=[place, place, pl.BlockSpec(memory_space=pltpu.HBM)],
        out_specs=place,
        out_shape=jax.ShapeDtypeStruct(total.shape, jnp.bfloat16),
        scratch_shapes=[pltpu.VMEM((TOKENS, WIDTH), jnp.bfloat16), pltpu.SemaphoreType.DMA((PIECES,))],
        compiler_params=pltpu.CompilerParams(vmem_limit_bytes=32 * 2**20),
        cost_estimate=pl.CostEstimate(flops=TOKENS * 1024 * 1024, bytes_accessed=8 * 2**20, transcendentals=0),
        name="project_near",
    )(total, weights, tokens)


def add_up_kernel(parts, mine, theirs):
    part = PAIRS * ROWS
    totals = []
    for x in range(2):
        total = parts[x].astype(jnp.float32)
        for y in range(1, PAIRS):
            total = total + parts[2 * y + x].astype(jnp.float32)
        totals.append(total)
    for q in range(4):
        to = theirs if q < 2 else mine
        pieces = [totals[x][:, q * part + y * ROWS : q * part + (y + 1) * ROWS] for y in range(PAIRS) for x in range(2)]
        to[:, pl.ds(q % 2 * 2 * part, 2 * part)] = jnp.concatenate(pieces, axis=1).astype(to.dtype)


def add_up(parts):
    shape = (parts.shape[1], parts.shape[2])
    return pl.pallas_call(
        add_up_kernel,
        out_shape=[jax.ShapeDtypeStruct(shape, jnp.float32), jax.ShapeDtypeStruct(shape, jnp.bfloat16)],
        compiler_params=pltpu.CompilerParams(vmem_limit_bytes=32 * 2**20),
        cost_estimate=pl.CostEstimate(flops=2**21, bytes_accessed=3 * 2**20, transcendentals=0),
        name="add_up",
    )(parts)


def shrink_kernel(first, second, tokens, out, *rest):
    a = [block[:, pl.ds(WIDTH, WIDTH)].astype(jnp.float32)[0:4] for block in (first, second)]
    a = jnp.concatenate(a, axis=0).astype(jnp.bfloat16)
    count = TOKENS // GROUPS
    step = pl.program_id(0) * tokens.shape[0]
    for k in range(tokens.shape[0]):
        for c, block in enumerate((first, second)):
            for h in range(4):
                out[step + k, pl.ds(c * 2 * ROWS + h * 16, 16), :] = block[:, pl.ds(h * RANK, RANK)]
        product = lax.dot_general(a, tokens[k], (((1,), (1,)), ((), ())), preferred_element_type=jnp.float32)
        high = jnp.concatenate([product[:, LANES:], jnp.zeros((8, 2 * LANES - count), jnp.float32)], axis=1)
        both = jnp.concatenate([product[:, :LANES], high], axis=0)
        out[step + k, pl.ds(4 * ROWS, 16), :] = both.astype(jnp.bfloat16)


def shrink(first, second, tokens, steps=2):
    side = pl.BlockSpec((16, 2 * WIDTH), lambda i: (HELD // 16, 0))
    columns = 4 * PAIRS * ROWS
    room = pl.BlockSpec(memory_space=pl.ANY)
    return pl.pallas_call(
        shrink_kernel,
        grid=(steps,),
        in_specs=[side, side, pl.BlockSpec((GROUPS // steps, TOKENS // GROUPS, WIDTH), lambda i: (i, 0, 0))],
        out_specs=[pl.BlockSpec((GROUPS, SIDE, LANES), lambda i: (0, 0, 0)), room, room],
        out_shape=[
            jax.ShapeDtypeStruct((GROUPS, SIDE, LANES), jnp.bfloat16),
            jax.ShapeDtypeStruct((TOKENS, columns), jnp.float32),
            jax.ShapeDtypeStruct((columns, WIDTH), jnp.bfloat16),
        ],
        compiler_params=pltpu.CompilerParams(vmem_limit_bytes=40 * 2**20),
        cost_estimate=pl.CostEstimate(flops=2**24, bytes_accessed=3 * 2**20, transcendentals=0),
        name="shrink",
    )(first, second, tokens.reshape(GROUPS, TOKENS // GROUPS, WIDTH))


def copies_kernel(side, out):
    total = side[0, pl.ds(4 * ROWS, 16), :].astype(jnp.float32)
    for k in range(1, GROUPS):
        total = total + side[k, pl.ds(4 * ROWS, 16), :].astype(jnp.float32)
    for place in range(out.shape[0]):
        out[place] = total.astype(jnp.bfloat16)


def copies_of(side, count):
    return pl.pallas_call(
        copies_kernel,
        out_shape=jax.ShapeDtypeStruct((count, 16, LANES), jnp.bfloat16),
        cost_estimate=pl.CostEstimate(flops=2**14, bytes_accessed=2**19, transcendentals=0),
        name="copies",
    )(side)


def spread_kernel(side, out):
    rank = lax.broadcasted_iota(jnp.int32, (RANK, 2 * RANK), 0)
    place = lax.broadcasted_iota(jnp.int32, (RANK, 2 * RANK), 1)
    slot = place // 4
    owner = slot // 2 % 2 * 32 + slot // 4 * 2 + slot % 2
    for q in range(4):
        hit = (place % 4 // 2 == q % 2) & (owner * 2 + place % 2 == rank)
        factor = jnp.concatenate([side[k, pl.ds(q * ROWS, ROWS), :] for k in range(GROUPS)], axis=0)
        out[q] = jnp.dot(
            factor, hit.astype(jnp.float32).astype(jnp.bfloat16), preferred_element_type=jnp.float32
        ).astype(jnp.bfloat16)


def spread_out(side):
    return pl.pallas_call(
        spread_kernel,
        out_shape=jax.ShapeDtypeStruct((4, GROUPS * ROWS, 2 * RANK), jnp.bfloat16),
        compiler_params=pltpu.CompilerParams(vmem_limit_bytes=16 * 2**20),
        cost_estimate=pl.CostEstimate(flops=2**26, bytes_accessed=2**20, transcendentals=0),
        name="spread_out",
    )(side)


def grow_kernel(factors, shrunk, mine, theirs):
    count = TOKENS // GROUPS
    values = shrunk[...].astype(jnp.float32)
    low = values[:, 0:8, :].reshape(2 * RANK, LANES).T.astype(jnp.bfloat16)
    high = values[:, 8:16, :].reshape(2 * RANK, LANES).T.astype(jnp.bfloat16)
    half = GROUPS * ROWS
    for q in range(4):
        to = mine if q < 2 else theirs
        columns = pl.ds(q % 2 * half, half)
        to[pl.ds(0, LANES), columns] = lax.dot_general(
            low, factors[q], (((1,), (1,)), ((), ())), preferred_element_type=jnp.float32
        ).astype(to.dtype)
        to[pl.ds(LANES, count - LANES), columns] = lax.dot_general(
            high, factors[q], (((1,), (1,)), ((), ())), preferred_element_type=jnp.float32
        )[: count - LANES].astype(to.dtype)


def grow(factors, shrunk):
    shape = (TOKENS // GROUPS, 2 * GROUPS * ROWS)
    return pl.pallas_call(
        grow_kernel,
        out_shape=[jax.ShapeDtypeStruct(shape, jnp.float32), jax.ShapeDtypeStruct(shape, jnp.bfloat16)],
        compiler_params=pltpu.CompilerParams(vmem_limit_bytes=32 * 2**20),
        cost_estimate=pl.CostEstimate(flops=2**25, bytes_accessed=2**20, transcendentals=0),
        name="grow",
    )(factors, shrunk)


def finish_kernel(core, mine, both, out):
    half = GROUPS * ROWS
    other = both.at[1 - core[0]]
    gate = mine[:, :half] + other[:, :half].astype(jnp.float32)
    up = mine[:, half:] + other[:, half:].astype(jnp.float32)
    out[...] = (gate / (1.0 + jnp.exp(-gate)) * up).astype(jnp.bfloat16)


def finish(core, mine, both):
    vmem = pl.BlockSpec(memory_space=pltpu.VMEM)
    return pl.pallas_call(
        finish_kernel,
        in_specs=[pl.BlockSpec(memory_space=pltpu.SMEM), vmem, vmem],
        out_specs=vmem,
        out_shape=jax.ShapeDtypeStruct((TOKENS // GROUPS, GROUPS * ROWS), jnp.bfloat16),
        compiler_params=pltpu.CompilerParams(vmem_limit_bytes=32 * 2**20),
        cost_estimate=pl.CostEstimate(flops=2**20, bytes_accessed=3 * 2**19, transcendentals=2**16),
        name="finish",
    )(core, mine, both)


def exchange_weights(blocks, other, tokens):
    weights = jnp.concatenate([part[:HELD].reshape(PAIRS, 2 * ROWS, 2 * WIDTH) for part in (other, blocks)], axis=1)
    weights = lax.all_to_all(weights, "y", 0, 0, tiled=True)
    return tuple(project_own(weights, tokens))


def exchange_shrunk(blocks, other, tokens):
    side, total, weights = shrink(blocks, other, tokens)
    return total, weights, lax.all_to_all(side, TENSOR, 0, 0, tiled=True)


def base_term(total, weights, side, near_tokens):
    parts = project_near(total, weights, near_tokens)
    parts = lax.all_to_all(parts.reshape(GROUPS, TOKENS // GROUPS, -1), TENSOR, 0, 0, tiled=True)
    return tuple(add_up(parts))


def adapter_term(total, weights, side, near_tokens):
    copies = copies_of(side, lax.axis_size("xl") * lax.axis_size("z"))
    shrunk = lax.all_to_all(copies, ("z", "xl"), 0, 0, tiled=True)
    return tuple(grow(spread_out(side), shrunk))


def per_device(tokens, gate_ids, up_ids, gate_powers, up_powers, gate_b, up_b, gate_a, up_a):
    core = lax.axis_index("c").astype(jnp.int32)
    pairs = [(xl * 4 + 2 + xh, (1 - xl) * 4 + 2 + 1 - xh) for xl in range(2) for xh in range(2)]
    near_tokens = lax.ppermute(tokens, ("xl", "c", "xh"), pairs)
    own = lax.axis_index("xh").astype(jnp.int32).reshape(1)
    blocks = decode(own, gate_ids, up_ids, gate_powers, up_powers, gate_b, up_b, gate_a, up_a)
    other = lax.ppermute(blocks, "c", [(0, 1), (1, 0)])
    total, weights, side = lax.cond(core == 0, exchange_shrunk, exchange_weights, blocks, other, tokens)
    mine, theirs = lax.cond(core == 0, adapter_term, base_term, total, weights, side, near_tokens)
    return finish(core.reshape(1), mine, lax.all_gather(theirs, "c", axis=0))


def solution(mesh):
    split = Mesh(mesh.devices.reshape(2, 16, 2, 4, 2), ("xl", "z", "c", "y", "xh"))
    rows = P(FSDP + TENSOR, None)
    placed = (P(None, TENSOR), rows, rows, rows, rows, rows, rows, P(FSDP, TENSOR), P(FSDP, TENSOR))
    return jax.shard_map(per_device, mesh=split, in_specs=placed, out_specs=P(TENSOR, FSDP), check_vma=False)
```
